128 devices in a mesh: slab: 4 (over y), energy: 32 (over x, z, core).
Axes of the slice: x: 4, y: 4, z: 4, core: 2. Of those that a mesh axis runs over, the one named last changes fastest.
Arguments:
- g_lesser: float32 [2, 512, 131072], P(None, 'energy', 'slab'), may hold values from -6 to 6
- g_greater: float32 [2, 512, 131072], P(None, 'energy', 'slab'), may hold values from -6 to 6
- live_columns: int32 [131072], P('slab'), may hold values from 0 to 32767, as said below
- live_count: int32 [4], P('slab'), may hold values from 8192 to 16384, as said below
- mirror: int32 [131072], P('slab'), may hold values from 0 to 32767, as said below
Outputs:
- polar_lesser: float32 [2, 512, 131072], P(None, 'energy', 'slab')
The draws below stay inside these ranges and needn't reach their ends.
Inputs may be any that keep to these rules, and one draw needn't show every extreme that they name: `live_columns`: each slab's 32768 entries are a permutation of the slab's columns 0 .. 32767; the first live_count entries name its live pairs. `live_count`: A slab and its mirror-image slab (the one at the same place counted from the other end) hold equal counts; some slab holds exactly 16384 live pairs in every draw. Between a slab and its mirror-image slab the map is a bijection that is its own inverse and takes live pairs to live pairs.
All inputs are finite; a program needn't handle non-finite values.
Results may differ from the reference program's by a relative error of at most 0.0003.
Values sent between devices are 32-bit elements; how exact they have to be, the bound alone decides.
No kernel may reach another device: no remote copies, remote signals or barrier semaphores. Data moves between devices by JAX's collectives and lax.ppermute only.
A program may use at most 192 MiB of HBM per device.

```python
import math
import jax
import jax.numpy as jnp
from jax import lax

ENERGIES = 512
TRANSFORM = 1024
SLOTS_SLAB = 32768
LIVE_SLAB = 16384
PAIRS = 131072
N_SLAB = 4


def mirror_tables(key):
    slot_count = SLOTS_SLAB
    half_slabs = N_SLAB // 2
    counts_low = jax.random.randint(jax.random.fold_in(key, 11), (half_slabs,), LIVE_SLAB // 2, LIVE_SLAB + 1)
    chosen = jax.random.randint(jax.random.fold_in(key, 12), (), 0, half_slabs)
    counts_low = jnp.where(jnp.arange(half_slabs) == chosen, LIVE_SLAB, counts_low).astype(jnp.int32)
    counts = jnp.concatenate([counts_low, counts_low[::-1]]).astype(jnp.int32)
    columns = []
    for slab_index in range(N_SLAB):
        columns.append(jax.random.permutation(jax.random.fold_in(key, 100 + slab_index), slot_count).astype(jnp.int32))
    mirrors = [None] * N_SLAB
    for slab_index in range(half_slabs):
        partner = N_SLAB - 1 - slab_index
        shuffle = jax.random.permutation(jax.random.fold_in(key, 200 + slab_index), slot_count).astype(jnp.int32)
        sort_keys = jnp.where(jnp.arange(slot_count, dtype=jnp.int32) >= counts[slab_index], slot_count, 0) + shuffle
        ordering = jnp.argsort(sort_keys, stable=True).astype(jnp.int32)
        target = columns[partner][ordering]
        mirrors[slab_index] = jnp.zeros((slot_count,), jnp.int32).at[columns[slab_index]].set(target)
        mirrors[partner] = jnp.zeros((slot_count,), jnp.int32).at[target].set(columns[slab_index])
    return (counts, jnp.concatenate(columns), jnp.concatenate(mirrors))


def draw_live_count(key, part):
    return mirror_tables(key)[0]


def draw_live_columns(key, part):
    return mirror_tables(key)[1]


def draw_mirror(key, part):
    return mirror_tables(key)[2]


def shard_levels(stream_key, dims, cuts, low, largest):
    def one(dim, shards_of):
        heights = jax.random.uniform(jax.random.fold_in(jax.random.fold_in(stream_key, 6), dim), (shards_of,), jnp.float32, low / len(cuts), largest / len(cuts))
        return jnp.repeat(jnp.exp(heights), dims[dim] // shards_of).reshape((-1,) + (1,) * (len(dims) - dim - 1))

    level = one(*cuts[0])
    for cut in cuts[1:]:
        level = level * one(*cut)
    return level


def noise(stream_key, dims, scale, most, shards=(), kind=jnp.bfloat16):
    loudness = shard_levels(stream_key, dims, shards, -0.22, 0.18) if shards else 1.0
    drawn = jax.random.normal(stream_key, dims, jnp.float32) * scale * loudness
    return jnp.minimum(jnp.maximum(drawn, -most), most).astype(kind)


def setup_inputs(seed: int = 0) -> dict:
    arg_keys = jax.random.split(jax.random.key(seed), 6)
    g_lesser = noise(arg_keys[0], (2, ENERGIES, PAIRS), 1.0, 6.0, ((1, 32), (2, 4)), jnp.float32)
    g_greater = noise(arg_keys[1], (2, ENERGIES, PAIRS), 1.0, 6.0, ((1, 32), (2, 4)), jnp.float32)
    live_columns = draw_live_columns(jax.random.fold_in(arg_keys[5], 71), 0)
    live_count = draw_live_count(jax.random.fold_in(arg_keys[5], 71), 0)
    mirror = draw_mirror(jax.random.fold_in(arg_keys[5], 71), 0)
    return {"g_lesser": g_lesser, "g_greater": g_greater, "live_columns": live_columns, "live_count": live_count, "mirror": mirror}


def reference(g_lesser, g_greater, live_columns, live_count, mirror):
    slab_of = jnp.arange(PAIRS, dtype=jnp.int32) // SLOTS_SLAB
    partner_cols = (N_SLAB - 1 - slab_of) * SLOTS_SLAB + mirror
    offsets = slab_of * SLOTS_SLAB
    position = jnp.zeros((PAIRS,), jnp.int32).at[offsets + live_columns].set(jnp.arange(PAIRS, dtype=jnp.int32) % SLOTS_SLAB)
    is_live = position < live_count[slab_of]
    factor = 1.0 / math.sqrt(ENERGIES)

    def one_slab(slab_index):
        first_col = (slab_index * SLOTS_SLAB).astype(jnp.int32)
        own_rows = lax.dynamic_slice_in_dim(g_lesser, first_col, SLOTS_SLAB, 2)
        mirror_cols = lax.dynamic_slice_in_dim(partner_cols, first_col, SLOTS_SLAB, 0)
        other_rows = jnp.take(g_greater, mirror_cols, axis=2)
        lesser_c = own_rows[0] + 1j * own_rows[1]
        greater_conj = other_rows[0] - 1j * other_rows[1]
        lesser_f = jnp.fft.fft(lesser_c, n=TRANSFORM, axis=0)
        greater_f = jnp.conj(jnp.fft.fft(greater_conj, n=TRANSFORM, axis=0))
        correlation = jnp.fft.ifft(lesser_f * greater_f, axis=0)[:ENERGIES]
        part_re = factor * jnp.imag(correlation)
        part_im = -factor * jnp.real(correlation)
        return jnp.stack([part_re, part_im]).astype(jnp.float32)
    per_slab = lax.map(one_slab, jnp.arange(N_SLAB, dtype=jnp.int32))
    result = jnp.moveaxis(per_slab, 0, 2).reshape(2, ENERGIES, PAIRS)
    return jnp.where(is_live[None, None, :], result, jnp.zeros_like(result))
```

```python
import functools
import math

import jax
import jax.numpy as jnp
import ml_dtypes
import numpy as np
from jax import lax
from jax.experimental import pallas as pl
from jax.experimental.pallas import tpu as pltpu

F32 = jnp.float32
BF16 = jnp.bfloat16
SLOTS = 32768
LIVE = 16384
ENERGIES = 512
PARTS = 32
WIDTHS = (256, 256)
VMEM_BYTES = 40 << 20
SMEM = pl.BlockSpec(memory_space=pltpu.SMEM)
VMEM = pl.BlockSpec(memory_space=pltpu.VMEM)
UNROLL = 32


def params():
    return pltpu.CompilerParams(vmem_limit_bytes=VMEM_BYTES)


def rows_kernel(a_low, b_low, a_high, b_high, rows):
    for j in range(a_low.shape[-1] // 128):
        s = slice(j * 128, (j + 1) * 128)
        block = [ref[:, :, s].reshape(32, 128) for ref in (a_low, b_low, a_high, b_high)]
        rows[s, :] = jnp.concatenate(block, 0).T


def column_rows(a, b, block=2048):
    steps = LIVE // block
    low = pl.BlockSpec((2, 16, block), lambda i: (0, 0, i))
    high = pl.BlockSpec((2, 16, block), lambda i: (0, 0, i + steps))
    return pl.pallas_call(
        rows_kernel,
        grid=(steps,),
        in_specs=[low, low, high, high],
        out_specs=pl.BlockSpec((block, 128), lambda i: (i, 0)),
        out_shape=jax.ShapeDtypeStruct((LIVE, 128), F32),
        compiler_params=params(),
        name="column_rows",
    )(a, b, a, b)


def gather_kernel(count, order, table, rows, out, packed, *, base, width):
    half = lax.broadcasted_iota(jnp.int32, (1, 128), 1) >> 6

    def step(k, _):
        first = pl.multiple_of(k * UNROLL, UNROLL)
        cols = [table[order[first + u]] for u in range(UNROLL)]
        picked = [rows[pl.ds(c & (LIVE - 1), 1), :] for c in cols]
        for u in range(UNROLL):
            mine = (jnp.full((1, 128), cols[u], jnp.int32) >> 14) == half
            packed[pl.ds(first + u, 1), :] = jnp.where(mine, picked[u], 0.0)
        return 0

    lax.fori_loop(0, PARTS * width // UNROLL, step, 0)
    lane = lax.broadcasted_iota(jnp.int32, (1, 128), 1)

    def turn(j, _):
        for w in range(width // 128):
            first = pl.multiple_of(j * width + w * 128, 128)
            block = packed[pl.ds(first, 128), :].T
            block = block[:64] + block[64:]
            out[j, :, w * 128 : (w + 1) * 128] = jnp.where(lane + first + base < count[0], block, 0.0)
        return 0

    lax.fori_loop(0, PARTS, turn, 0)


def gather(count, order, table, rows, base, width):
    items = PARTS * width
    return pl.pallas_call(
        functools.partial(gather_kernel, base=base, width=width),
        in_specs=[SMEM, SMEM, SMEM, VMEM],
        out_specs=VMEM,
        out_shape=jax.ShapeDtypeStruct((PARTS, 64, width), F32),
        scratch_shapes=[pltpu.VMEM((items, 128), F32)],
        compiler_params=params(),
        cost_estimate=pl.CostEstimate(flops=items * 2000, bytes_accessed=items * 4000, transcendentals=0),
        name="gather",
    )(count, order, table, rows)


def columns_kernel(order, table, out):
    def step(k, _):
        first = pl.multiple_of(k * UNROLL, UNROLL)
        cols = [table[order[first + u]] for u in range(UNROLL)]
        for u in range(UNROLL):
            out[first + u] = cols[u]
        return 0

    lax.fori_loop(0, LIVE // UNROLL, step, 0)


def columns_in_order(order, table):
    return pl.pallas_call(
        columns_kernel,
        in_specs=[SMEM, SMEM],
        out_specs=SMEM,
        out_shape=jax.ShapeDtypeStruct((LIVE,), jnp.int32),
        cost_estimate=pl.CostEstimate(flops=LIVE * 1000, bytes_accessed=LIVE * 2000, transcendentals=0),
        name="columns_in_order",
    )(order, table)


def tables():
    n = np.arange(256)
    angle = 2.0 * np.pi * ((n[:, None] * n[None, :]) % 256) / 256.0
    matrix = np.concatenate([np.cos(angle), np.sin(angle)], 0).astype(np.float32)
    high = matrix.astype(ml_dtypes.bfloat16)
    low = (matrix - high.astype(np.float32)).astype(ml_dtypes.bfloat16)
    matrix = np.concatenate([high, high, low], 1)
    phase = 2.0 * np.pi * np.arange(1, 4)[:, None] * n[None, :] / 1024.0
    turn = np.stack([np.cos(phase), np.sin(phase)], 1).astype(np.float32)
    return matrix, np.repeat(turn[:, :, :, None], 128, 3)


def split(values):
    high = values.astype(BF16)
    low = (values - high.astype(F32)).astype(BF16)
    return jnp.concatenate([high, low, high], 0)


def correlate_kernel(matrix, turn, a_ref, b_ref, out):
    scale = 1.0 / (1024.0 * math.sqrt(ENERGIES))

    def tile(w, _):
        lanes = pl.ds(pl.multiple_of(w * 128, 128), 128)

        def halves(ref, part):
            values = ref[:, part * 16 : part * 16 + 16, lanes].reshape(ENERGIES, 128)
            return values[:256], values[256:]

        ar0, ar1 = halves(a_ref, 0)
        ai0, ai1 = halves(a_ref, 1)
        br0, br1 = halves(b_ref, 0)
        bi0, bi1 = halves(b_ref, 1)
        low_re = low_im = high_re = high_im = None
        for r in range(4):
            if r == 0:
                ur, ui, vr, vi = ar0 + ar1, ai0 + ai1, br0 + br1, bi0 + bi1
            elif r == 1:
                ur, ui, vr, vi = ar0 + ai1, ai0 - ar1, br0 - bi1, bi0 + br1
            elif r == 2:
                ur, ui, vr, vi = ar0 - ar1, ai0 - ai1, br0 - br1, bi0 - bi1
            else:
                ur, ui, vr, vi = ar0 - ai1, ai0 + ar1, br0 + bi1, bi0 - br1
            if r:
                c, s = turn[r - 1, 0], turn[r - 1, 1]
                ur, ui = ur * c + ui * s, ui * c - ur * s
                vr, vi = vr * c - vi * s, vi * c + vr * s
            spec = jnp.dot(
                matrix[...],
                split(jnp.concatenate([ur, ui, vr, vi], 1)),
                preferred_element_type=F32,
            )
            cos, sin = spec[:256], spec[256:]
            a_re = cos[:, :128] + sin[:, 128:256]
            a_im = cos[:, 128:256] - sin[:, :128]
            b_re = cos[:, 256:384] - sin[:, 384:]
            b_im = cos[:, 384:] + sin[:, 256:384]
            p_re = a_re * b_re - a_im * b_im
            p_im = a_re * b_im + a_im * b_re
            back = jnp.dot(
                matrix[...], split(jnp.concatenate([p_re, p_im], 1)), preferred_element_type=F32
            )
            q_re = back[:256, :128] - back[256:, 128:]
            q_im = back[:256, 128:] + back[256:, :128]
            if r:
                q_re, q_im = q_re * c - q_im * s, q_re * s + q_im * c
            if r == 0:
                low_re, low_im, high_re, high_im = q_re, q_im, q_re, q_im
            else:
                low_re, low_im = low_re + q_re, low_im + q_im
                if r == 1:
                    high_re, high_im = high_re - q_im, high_im + q_re
                elif r == 2:
                    high_re, high_im = high_re - q_re, high_im - q_im
                else:
                    high_re, high_im = high_re + q_im, high_im - q_re
        out[:16, :16, lanes] = (low_im * scale).reshape(16, 16, 128)
        out[16:, :16, lanes] = (high_im * scale).reshape(16, 16, 128)
        out[:16, 16:, lanes] = (low_re * -scale).reshape(16, 16, 128)
        out[16:, 16:, lanes] = (high_re * -scale).reshape(16, 16, 128)
        return 0

    lax.fori_loop(0, a_ref.shape[-1] // 128, tile, 0)


def correlate(matrix, turn, a, b):
    width = a.shape[-1]
    return pl.pallas_call(
        correlate_kernel,
        in_specs=[VMEM] * 4,
        out_specs=VMEM,
        out_shape=jax.ShapeDtypeStruct((PARTS, 32, width), F32),
        compiler_params=params(),
        cost_estimate=pl.CostEstimate(
            flops=width * 2 * 4 * 512 * 768 * 6, bytes_accessed=width * 12288, transcendentals=0
        ),
        name="correlate",
    )(matrix, turn, a, b)


def scatter_kernel(*refs, width, first_chunk):
    if first_chunk:
        where, values, out, rows = refs
        out[...] = jnp.zeros_like(out)
    else:
        where, values, before, out, rows = refs
        out[...] = before[...]
    group = lax.broadcasted_iota(jnp.int32, (1, 128), 1) >> 5

    def turn(j, _):
        for w in range(width // 128):
            first = pl.multiple_of(j * width + w * 128, 128)
            block = values[j, :, w * 128 : (w + 1) * 128]
            rows[pl.ds(first, 128), :] = jnp.concatenate([block] * 4, 0).T
        return 0

    lax.fori_loop(0, PARTS, turn, 0)

    def step(k, _):
        first = pl.multiple_of(k * UNROLL, UNROLL)
        places = [where[first + u] for u in range(UNROLL)]
        picked = [rows[pl.ds(first + u, 1), :] for u in range(UNROLL)]
        for u in range(UNROLL):
            mine = (jnp.full((1, 128), places[u], jnp.int32) >> 13) == group
            pltpu.store(out.at[pl.ds(places[u] & 8191, 1), :], picked[u], mask=mine)
        return 0

    lax.fori_loop(0, PARTS * width // UNROLL, step, 0)


def scatter(where, values, before):
    width = values.shape[-1]
    items = PARTS * width
    operands = (where, values) if before is None else (where, values, before)
    return pl.pallas_call(
        functools.partial(scatter_kernel, width=width, first_chunk=before is None),
        in_specs=[SMEM] + [VMEM] * (len(operands) - 1),
        out_specs=VMEM,
        out_shape=jax.ShapeDtypeStruct((SLOTS // 4, 128), F32),
        scratch_shapes=[pltpu.VMEM((items, 128), F32)],
        compiler_params=params(),
        cost_estimate=pl.CostEstimate(flops=items * 1000, bytes_accessed=items * 2500, transcendentals=0),
        name="scatter",
    )(*operands)


def slots_kernel(rows, out):
    for q in range(rows.shape[0] // 128):
        block = rows[q * 128 : (q + 1) * 128, :].T
        for g in range(4):
            s = slice(q * 512 + g * 128, q * 512 + (g + 1) * 128)
            out[:, :, s] = block[g * 32 : (g + 1) * 32].reshape(2, 16, 128)


def to_slots(rows, block=1024):
    return pl.pallas_call(
        slots_kernel,
        grid=(SLOTS // 4 // block,),
        in_specs=[pl.BlockSpec((block, 128), lambda i: (i, 0))],
        out_specs=pl.BlockSpec((2, 16, 4 * block), lambda i: (0, 0, i)),
        out_shape=jax.ShapeDtypeStruct((2, 16, SLOTS), F32),
        compiler_params=params(),
        name="to_slots",
    )(rows)


def local(g_lesser, g_greater, live_columns, live_count, mirror):
    slabs = lax.axis_size("slab")
    across = [(s, slabs - 1 - s) for s in range(slabs)]
    is_upper = lax.axis_index("slab") >= slabs // 2
    own = jnp.concatenate([live_columns[:LIVE], mirror])
    other = lax.ppermute(own, "slab", across)
    order = jnp.where(is_upper, other[:LIVE], live_columns[:LIVE])
    table = jnp.where(is_upper, other[LIVE:], jnp.arange(SLOTS, dtype=jnp.int32))
    matrix, turn = tables()
    matrix, turn = jnp.asarray(matrix), jnp.asarray(turn)

    rows = column_rows(g_lesser, g_greater)
    bases = np.cumsum((0,) + WIDTHS) * PARTS
    polar = []
    for k, width in enumerate(WIDTHS):
        base = int(bases[k])
        picked = gather(live_count, order[base : base + PARTS * width], table, rows, base, width)
        arrived = lax.all_to_all(picked, "energy", 0, 0, tiled=True)
        mirrored = lax.ppermute(arrived[:, 32:], "slab", across)
        result = correlate(matrix, turn, arrived[:, :32], mirrored)
        polar.append(lax.all_to_all(result, "energy", 0, 0, tiled=True))
    cols = columns_in_order(order, table)
    where = (cols >> 9 << 7) | (cols & 127) | ((cols >> 7 & 3) << 13)
    slots = None
    for k, width in enumerate(WIDTHS):
        base = int(bases[k])
        slots = scatter(where[base : base + PARTS * width], polar[k], slots)
    return to_slots(slots)


def solution(mesh):
    spec = jax.P(None, "energy", "slab")
    return jax.shard_map(
        local,
        mesh=mesh,
        in_specs=(spec, spec, jax.P("slab"), jax.P("slab"), jax.P("slab")),
        out_specs=spec,
        check_vma=False,
    )
```

```python
import functools
import math

import jax
import jax.numpy as jnp
import ml_dtypes
import numpy as np
from jax import lax
from jax.experimental import pallas as pl
from jax.experimental.pallas import tpu as pltpu

F32 = jnp.float32
BF16 = jnp.bfloat16
SLOTS = 32768
LIVE = 16384
ENERGIES = 512
PARTS = 32
WIDTHS = (256, 256)
VMEM_BYTES = 60 << 20
SMEM = pl.BlockSpec(memory_space=pltpu.SMEM)
VMEM = pl.BlockSpec(memory_space=pltpu.VMEM)
ANY = pl.BlockSpec(memory_space=pl.ANY)
UNROLL = 32


def params(limit=VMEM_BYTES):
    return pltpu.CompilerParams(vmem_limit_bytes=limit)


def cost(flops, bytes_accessed):
    return pl.CostEstimate(flops=flops, bytes_accessed=bytes_accessed, transcendentals=0)


def rows_kernel(a_low, b_low, a_high, b_high, rows):
    first_half = lax.broadcasted_iota(jnp.int32, (128, 128), 1) < 64
    for j in range(a_low.shape[-1] // 128):
        s = slice(j * 128, (j + 1) * 128)
        block = [ref[:, :, s].reshape(32, 128) for ref in (a_low, b_low, a_high, b_high)]
        block = jnp.concatenate(block, 0).T
        rows[0, s, :] = jnp.where(first_half, block, 0.0)
        rows[1, s, :] = jnp.where(first_half, 0.0, block)


def column_rows(a, b, block=1024):
    steps = LIVE // block
    low = pl.BlockSpec((2, 16, block), lambda i: (0, 0, i))
    high = pl.BlockSpec((2, 16, block), lambda i: (0, 0, i + steps))
    rows = pl.pallas_call(
        rows_kernel,
        grid=(steps,),
        in_specs=[low, low, high, high],
        out_specs=pl.BlockSpec((2, block, 128), lambda i: (0, i, 0)),
        out_shape=jax.ShapeDtypeStruct((2, LIVE, 128), F32),
        compiler_params=params(),
        cost_estimate=cost(1 << 20, 24 << 20),
        name="column_rows",
    )(a, b, a, b)
    return rows.reshape(SLOTS, 128)


def gather_kernel(count, order, table, rows, out, *rest, base, width):
    places, even, odd = rest if len(rest) == 3 else (None, *rest)
    per = width // 128
    lane = lax.broadcasted_iota(jnp.int32, (1, 128), 1)

    def fill(block, packed):
        for k in range(0, 128, UNROLL):
            first = pl.multiple_of(block * 128 + k, UNROLL)
            cols = [table[order[first + u]] for u in range(UNROLL)]
            if places is not None:
                for u in range(UNROLL):
                    places[first + u] = cols[u]
            for u in range(UNROLL):
                packed[k + u : k + u + 1, :] = rows[pl.ds(cols[u], 1), :]

    def turn(j, w, packed):
        block = packed[...].T
        live = lane + (j * width + w * 128 + base) < count[0]
        out[j, :, w * 128 : (w + 1) * 128] = jnp.where(live, block[:64] + block[64:], 0.0)

    fill(0, even)
    bufs = (even, odd)

    def step(k, _):
        for h in range(2):
            for w in range(per):
                now = h * per + w
                turn(2 * k + h, w, bufs[now % 2])
                fill(jnp.minimum(2 * k * per + now + 1, PARTS * per - 1), bufs[(now + 1) % 2])
        return 0

    lax.fori_loop(0, PARTS // 2, step, 0)


def gather(count, order, table, rows, base, width, with_places):
    items = PARTS * width
    out_shape = [jax.ShapeDtypeStruct((PARTS, 64, width), F32)]
    out_specs = [VMEM]
    if with_places:
        out_shape.append(jax.ShapeDtypeStruct((items,), jnp.int32))
        out_specs.append(SMEM)
    return pl.pallas_call(
        functools.partial(gather_kernel, base=base, width=width),
        in_specs=[SMEM, SMEM, SMEM, VMEM],
        out_specs=out_specs,
        out_shape=out_shape,
        scratch_shapes=[pltpu.VMEM((128, 128), F32)] * 2,
        compiler_params=params(),
        cost_estimate=cost(items * 2000, items * 5000),
        name="gather",
    )(count, order, table, rows)


def columns_kernel(order, table, _, out):
    def step(k, _):
        for v in range(0, UNROLL, 8):
            first = pl.multiple_of(k * UNROLL + v, 8)
            cols = [table[order[first + u]] for u in range(8)]
            for u in range(8):
                out[first + u] = cols[u]
        return 0

    lax.fori_loop(0, out.shape[0] // UNROLL, step, 0)


def columns_in_order(order, table, after):
    items = order.shape[0]
    return pl.pallas_call(
        columns_kernel,
        in_specs=[SMEM, SMEM, ANY],
        out_specs=SMEM,
        out_shape=jax.ShapeDtypeStruct((items,), jnp.int32),
        compiler_params=params(2 << 20),
        cost_estimate=cost(items * 2000, items * 5000),
        name="columns_in_order",
    )(order, table, after)


def tables():
    n = np.arange(256)
    angle = 2.0 * np.pi * ((n[:, None] * n[None, :]) % 256) / 256.0
    matrix = np.concatenate([np.cos(angle), np.sin(angle)], 0).astype(np.float32)
    high = matrix.astype(ml_dtypes.bfloat16)
    low = (matrix - high.astype(np.float32)).astype(ml_dtypes.bfloat16)
    matrix = np.concatenate([high, high, low], 1)
    phase = 2.0 * np.pi * np.arange(1, 4)[:, None] * n[None, :] / 1024.0
    turn = np.stack([np.cos(phase), np.sin(phase)], 1).astype(np.float32)
    return matrix, np.repeat(turn[:, :, :, None], 128, 3)


def split(values):
    high = values.astype(BF16)
    low = (values - high.astype(F32)).astype(BF16)
    return jnp.concatenate([high, low, high], 0)


def correlate_kernel(matrix, turn, a_ref, b_ref, *rest):
    out = rest[-1]
    scale = 1.0 / (1024.0 * math.sqrt(ENERGIES))

    def tile(w, _):
        lanes = pl.ds(pl.multiple_of(w * 128, 128), 128)

        def halves(ref, part):
            values = ref[:, part * 16 : part * 16 + 16, lanes].reshape(ENERGIES, 128)
            return values[:256], values[256:]

        ar0, ar1 = halves(a_ref, 0)
        ai0, ai1 = halves(a_ref, 1)
        br0, br1 = halves(b_ref, 0)
        bi0, bi1 = halves(b_ref, 1)
        low_re = low_im = high_re = high_im = None
        for r in range(4):
            if r == 0:
                ur, ui, vr, vi = ar0 + ar1, ai0 + ai1, br0 + br1, bi0 + bi1
            elif r == 1:
                ur, ui, vr, vi = ar0 + ai1, ai0 - ar1, br0 - bi1, bi0 + br1
            elif r == 2:
                ur, ui, vr, vi = ar0 - ar1, ai0 - ai1, br0 - br1, bi0 - bi1
            else:
                ur, ui, vr, vi = ar0 - ai1, ai0 + ar1, br0 + bi1, bi0 - br1
            if r:
                c, s = turn[r - 1, 0], turn[r - 1, 1]
                ur, ui = ur * c + ui * s, ui * c - ur * s
                vr, vi = vr * c - vi * s, vi * c + vr * s
            spec = jnp.dot(
                matrix[...],
                split(jnp.concatenate([ur, ui, vr, vi], 1)),
                preferred_element_type=F32,
            )
            cos, sin = spec[:256], spec[256:]
            a_re = cos[:, :128] + sin[:, 128:256]
            a_im = cos[:, 128:256] - sin[:, :128]
            b_re = cos[:, 256:384] - sin[:, 384:]
            b_im = cos[:, 384:] + sin[:, 256:384]
            p_re = a_re * b_re - a_im * b_im
            p_im = a_re * b_im + a_im * b_re
            back = jnp.dot(
                matrix[...], split(jnp.concatenate([p_re, p_im], 1)), preferred_element_type=F32
            )
            q_re = back[:256, :128] - back[256:, 128:]
            q_im = back[:256, 128:] + back[256:, :128]
            if r:
                q_re, q_im = q_re * c - q_im * s, q_re * s + q_im * c
            if r == 0:
                low_re, low_im, high_re, high_im = q_re, q_im, q_re, q_im
            else:
                low_re, low_im = low_re + q_re, low_im + q_im
                if r == 1:
                    high_re, high_im = high_re - q_im, high_im + q_re
                elif r == 2:
                    high_re, high_im = high_re - q_re, high_im - q_im
                else:
                    high_re, high_im = high_re + q_im, high_im - q_re
        out[:16, :16, lanes] = (low_im * scale).reshape(16, 16, 128)
        out[16:, :16, lanes] = (high_im * scale).reshape(16, 16, 128)
        out[:16, 16:, lanes] = (low_re * -scale).reshape(16, 16, 128)
        out[16:, 16:, lanes] = (high_re * -scale).reshape(16, 16, 128)
        return 0

    lax.fori_loop(0, a_ref.shape[-1] // 128, tile, 0)


def correlate(matrix, turn, a, b, *after):
    width = a.shape[-1]
    return pl.pallas_call(
        correlate_kernel,
        in_specs=[VMEM] * 4 + [ANY] * len(after),
        out_specs=VMEM,
        out_shape=jax.ShapeDtypeStruct((PARTS, 32, width), F32),
        compiler_params=params(24 << 20),
        cost_estimate=cost(width * 2 * 4 * 512 * 768 * 6, width * 12288),
        name="correlate",
    )(matrix, turn, a, b, *after)


def greater_kernel(both, _, out, sem):
    copy = pltpu.make_async_copy(both.at[:, 32:, :], out, sem)
    copy.start()
    copy.wait()


def greater_part(both, after):
    shape = (PARTS, 32, both.shape[-1])
    return pl.pallas_call(
        greater_kernel,
        in_specs=[ANY, ANY],
        out_specs=ANY,
        out_shape=jax.ShapeDtypeStruct(shape, F32),
        scratch_shapes=[pltpu.SemaphoreType.DMA],
        compiler_params=params(1 << 20),
        cost_estimate=cost(1 << 20, 4 << 20),
        name="greater_part",
    )(both, after)


def scatter_rows(row_of, column, values, out, even, odd, width):
    per = width // 128

    def turn(block, packed):
        j, w = block // per, block % per
        lanes = pl.ds(pl.multiple_of(w * 128, 128), 128)
        group = (column[pl.ds(block, 1), :] >> 7) & 3
        data = values[j, :, lanes]
        packed[...] = jnp.concatenate([jnp.where(group == g, data, 0.0) for g in range(4)], 0).T

    def spread(block, packed):
        for k in range(0, 128, UNROLL):
            first = pl.multiple_of(block * 128 + k, UNROLL)
            rows = [row_of[first + u] for u in range(UNROLL)]
            for u in range(UNROLL):
                row = packed[k + u : k + u + 1, :]
                pltpu.store(out.at[pl.ds(rows[u], 1), :], row, mask=row != 0.0)

    turn(0, even)

    def step(k, _):
        turn(2 * k + 1, odd)
        spread(2 * k, even)
        turn(jnp.minimum(2 * k + 2, PARTS * per - 1), even)
        spread(2 * k + 1, odd)
        return 0

    lax.fori_loop(0, PARTS * per // 2, step, 0)


def scatter_first_kernel(row_of, column, values, out, even, odd, slots, sem):
    slots[...] = jnp.zeros_like(slots)
    scatter_rows(row_of, column, values, slots, even, odd, values.shape[-1])
    save = pltpu.make_async_copy(slots, out.at[0], sem)
    save.start()
    save.wait()


def scatter_last_kernel(row_of, column, values, before, out, even, odd, slots, staged, in_sem, out_sem):
    load = pltpu.make_async_copy(before.at[0], slots, in_sem)
    load.start()
    load.wait()
    scatter_rows(row_of, column, values, slots, even, odd, values.shape[-1])
    pieces = out_sem.shape[0]
    span = SLOTS // pieces
    copies = []
    for p in range(pieces):
        for q in range(p * span // 512, (p + 1) * span // 512):
            block = slots[q * 128 : (q + 1) * 128, :].T
            for g in range(4):
                s = slice(q * 512 + g * 128, q * 512 + (g + 1) * 128)
                staged[:, :, s] = block[g * 32 : (g + 1) * 32].reshape(2, 16, 128)
        piece = slice(p * span, (p + 1) * span)
        copies.append(pltpu.make_async_copy(staged.at[:, :, piece], out.at[:, :, piece], out_sem.at[p]))
        copies[-1].start()
    for copy in copies:
        copy.wait()


def scatter(columns, values, before):
    width = values.shape[-1]
    items = PARTS * width
    row_of = (columns >> 9 << 7) | (columns & 127)
    column = columns.reshape(items // 128, 128)
    first = before is None
    scratch = [
        pltpu.VMEM((128, 128), F32),
        pltpu.VMEM((128, 128), F32),
        pltpu.VMEM((SLOTS // 4, 128), F32),
    ]
    if first:
        scratch += [pltpu.SemaphoreType.DMA]
    else:
        scratch += [
            pltpu.VMEM((2, 16, SLOTS), F32),
            pltpu.SemaphoreType.DMA,
            pltpu.SemaphoreType.DMA((8,)),
        ]
    return pl.pallas_call(
        scatter_first_kernel if first else scatter_last_kernel,
        in_specs=[SMEM, VMEM, VMEM] + ([] if first else [ANY]),
        out_specs=ANY,
        out_shape=jax.ShapeDtypeStruct((6, SLOTS // 4, 128) if first else (2, 16, SLOTS), F32),
        scratch_shapes=scratch,
        compiler_params=params(44 << 20),
        cost_estimate=cost(items * 1000, items * 4000),
        name="scatter",
    )(row_of, column, values, *(() if first else (before,)))


def local(g_lesser, g_greater, live_columns, live_count, mirror):
    slabs = lax.axis_size("slab")
    across = [(s, slabs - 1 - s) for s in range(slabs)]
    is_upper = lax.axis_index("slab") >= slabs // 2
    other_mirror = lax.ppermute(mirror, "slab", across)
    other_live = lax.ppermute(live_columns[:LIVE], "slab", across)
    order = jnp.where(is_upper, other_live, live_columns[:LIVE])
    table = jnp.where(is_upper, other_mirror, jnp.arange(SLOTS, dtype=jnp.int32))
    matrix, turn = tables()
    matrix, turn = jnp.asarray(matrix), jnp.asarray(turn)

    rows = column_rows(g_lesser, g_greater)
    half = WIDTHS[0]
    orders = [order[: PARTS * half], order[PARTS * half :]]
    (picked0,) = gather(live_count, orders[0], table, rows, 0, half, False)
    picked1, columns1 = gather(live_count, orders[1], table, rows, PARTS * half, WIDTHS[1], True)
    columns0 = columns_in_order(orders[0], table, picked1)

    def swap(values):
        return lax.all_to_all(values, "energy", 0, 0, tiled=True)

    def mirrored(values, after):
        return lax.ppermute(greater_part(values, after), "slab", across)

    arrived0 = swap(picked0)
    arrived1 = swap(picked1)
    result0 = correlate(matrix, turn, arrived0, mirrored(arrived0, picked1), columns0)
    result1 = correlate(matrix, turn, arrived1, mirrored(arrived1, result0))
    polar0 = swap(result0)
    polar1 = swap(result1)
    slots = scatter(columns0, polar0, None)
    return scatter(columns1, polar1, slots)


def solution(mesh):
    spec = jax.P(None, "energy", "slab")
    return jax.shard_map(
        local,
        mesh=mesh,
        in_specs=(spec, spec, jax.P("slab"), jax.P("slab"), jax.P("slab")),
        out_specs=spec,
        check_vma=False,
    )
```

```python
import functools
import math

import jax
import jax.numpy as jnp
import ml_dtypes
import numpy as np
from jax import lax
from jax.experimental import pallas as pl
from jax.experimental.pallas import tpu as pltpu

F32 = jnp.float32
BF16 = jnp.bfloat16
SLOTS = 32768
LIVE = 16384
ENERGIES = 512
PARTS = 32
WIDTHS = (256, 256)
VMEM_BYTES = 60 << 20
SMEM = pl.BlockSpec(memory_space=pltpu.SMEM)
VMEM = pl.BlockSpec(memory_space=pltpu.VMEM)
ANY = pl.BlockSpec(memory_space=pl.ANY)
UNROLL = 32
BATCH = 4
TILE = 256


def params(limit=VMEM_BYTES):
    return pltpu.CompilerParams(vmem_limit_bytes=limit)


def cost(flops, bytes_accessed):
    return pl.CostEstimate(flops=flops, bytes_accessed=bytes_accessed, transcendentals=0)


def rows_kernel(a_low, b_low, a_high, b_high, rows):
    for j in range(a_low.shape[-1] // 128):
        s = slice(j * 128, (j + 1) * 128)
        block = [ref[:, :, s].reshape(32, 128) for ref in (a_low, b_low, a_high, b_high)]
        rows[s, :] = jnp.concatenate(block, 0).T


def column_rows(a, b, block=4096):
    steps = LIVE // block
    low = pl.BlockSpec((2, 16, block), lambda i: (0, 0, i))
    high = pl.BlockSpec((2, 16, block), lambda i: (0, 0, i + steps))
    return pl.pallas_call(
        rows_kernel,
        grid=(steps,),
        in_specs=[low, low, high, high],
        out_specs=pl.BlockSpec((block, 128), lambda i: (i, 0)),
        out_shape=jax.ShapeDtypeStruct((LIVE, 128), F32),
        compiler_params=params(),
        cost_estimate=cost(1 << 20, 24 << 20),
        name="column_rows",
    )(a, b, a, b)


def gather_kernel(count, order_in, map_in, rows, out, places, packed, order, mapped, table, sems, row_sems, *, base):
    width = out.shape[-1]
    per = width // 128
    copies = [
        pltpu.make_async_copy(map_in, mapped, sems.at[0]),
        pltpu.make_async_copy(order_in, order, sems.at[1]),
    ]
    parts = row_sems.shape[0]
    span = LIVE // parts
    loads = []
    for p in range(parts):
        s = pl.ds(p * span, span)
        loads.append(pltpu.make_async_copy(rows.at[s, :], table.at[s, :], row_sems.at[p]))
    for copy in copies + loads:
        copy.start()
    step = 2048
    first_half = lax.broadcasted_iota(jnp.int32, (8, 128), 1) < 64
    number = lax.broadcasted_iota(jnp.int32, (8, 128), 0).astype(F32)
    for p in range(parts):
        loads[p].wait()

        def widen(k, _):
            first = pl.multiple_of(p * span + k * step, step)
            offset = number + first.astype(F32)
            for r in range(0, step, 8):
                both = table[pl.ds(first + r, 8), :]
                high = pltpu.roll(both, 64, 1)
                column = offset + float(r)
                table[pl.ds(first + r, 8), :] = jnp.where(first_half, both, column)
                table[pl.ds(first + r + LIVE, 8), :] = jnp.where(first_half, high, column + float(LIVE))
            return 0

        lax.fori_loop(0, span // step, widen, 0)
    for copy in copies:
        copy.wait()
    lane = lax.broadcasted_iota(jnp.int32, (1, 128), 1)

    def batch(k, _):
        for r in range(0, BATCH * 128, UNROLL):
            first = pl.multiple_of(k * (BATCH * 128) + r, UNROLL)
            cols = [mapped[order[first + u]] for u in range(UNROLL)]
            for u in range(UNROLL):
                packed[r + u : r + u + 1, :] = table[pl.ds(cols[u], 1), :]
        blocks = [packed[b * 128 : (b + 1) * 128, :].T for b in range(BATCH)]
        for b in range(BATCH):
            block = k * BATCH + b
            w = b % per * 128
            live = lane + (block * 128 + base) < count[0]
            out[block // per, :, w : w + 128] = jnp.where(live, blocks[b][:64], 0.0)
            places[pl.ds(block, 1), :] = blocks[b][64:65].astype(jnp.int32)
        return 0

    lax.fori_loop(0, PARTS * per // BATCH, batch, 0)


def gather(count, order, table, rows, base, width):
    items = PARTS * width
    return pl.pallas_call(
        functools.partial(gather_kernel, base=base),
        in_specs=[SMEM, ANY, ANY, ANY],
        out_specs=[VMEM, VMEM],
        out_shape=[
            jax.ShapeDtypeStruct((PARTS, 64, width), F32),
            jax.ShapeDtypeStruct((items // 128, 128), jnp.int32),
        ],
        scratch_shapes=[
            pltpu.VMEM((BATCH * 128, 128), F32),
            pltpu.SMEM((items,), jnp.int32),
            pltpu.SMEM((SLOTS,), jnp.int32),
            pltpu.VMEM((SLOTS, 128), F32),
            pltpu.SemaphoreType.DMA((2,)),
            pltpu.SemaphoreType.DMA((4,)),
        ],
        compiler_params=params(),
        cost_estimate=cost(items * 2000, items * 5000),
        name="gather",
    )(count, order, table, rows)


def tables():
    n = np.arange(256)
    angle = 2.0 * np.pi * ((n[:, None] * n[None, :]) % 256) / 256.0
    matrix = np.concatenate([np.cos(angle), np.sin(angle)], 0).astype(np.float32)
    high = matrix.astype(ml_dtypes.bfloat16)
    low = (matrix - high.astype(np.float32)).astype(ml_dtypes.bfloat16)
    matrix = np.concatenate([high, high, low], 1)
    phase = 2.0 * np.pi * np.arange(1, 4)[:, None] * n[None, :] / 1024.0
    turn = np.stack([np.cos(phase), np.sin(phase)], 1).astype(np.float32)
    return matrix, np.repeat(turn[:, :, :, None], 128, 3)


def split(values):
    high = values.astype(BF16)
    low = (values - high.astype(F32)).astype(BF16)
    return jnp.concatenate([high, low, high], 0)


def halves(ref, part, lanes):
    values = ref[:, part * 16 : part * 16 + 16, lanes].reshape(ENERGIES, -1)
    return values[:256], values[256:]


def turned(turn, r, lanes):
    repeat = (lanes.stop - lanes.start) // 128
    return [jnp.concatenate([turn[r - 1, part]] * repeat, 1) for part in range(2)]


def product(matrix, re, im):
    both = jnp.dot(matrix[...], split(jnp.concatenate([re, im], 1)), preferred_element_type=F32)
    half = re.shape[1]
    return both[:256, :half], both[:256, half:], both[256:, :half], both[256:, half:]


def lesser_kernel(matrix, turn, both, spectrum):
    for w in range(0, both.shape[-1], TILE):
        lanes = slice(w, w + TILE)
        re0, re1 = halves(both, 0, lanes)
        im0, im1 = halves(both, 1, lanes)
        for r in range(4):
            re = (re0 + re1, re0 + im1, re0 - re1, re0 - im1)[r]
            im = (im0 + im1, im0 - re1, im0 - im1, im0 + re1)[r]
            if r:
                c, s = turned(turn, r, lanes)
                re, im = re * c + im * s, im * c - re * s
            cos_re, cos_im, sin_re, sin_im = product(matrix, re, im)
            spectrum[r, 0, :, lanes] = cos_re + sin_im
            spectrum[r, 1, :, lanes] = cos_im - sin_re


def lesser_spectrum(matrix, turn, both):
    width = both.shape[-1]
    return pl.pallas_call(
        lesser_kernel,
        in_specs=[VMEM] * 3,
        out_specs=VMEM,
        out_shape=jax.ShapeDtypeStruct((4, 2, 256, width), F32),
        compiler_params=params(),
        cost_estimate=cost(width * 2 * 4 * 512 * 768 * 2, width * 12288),
        name="lesser_spectrum",
    )(matrix, turn, both)


def correlate_kernel(matrix, turn, spectrum, b_ref, out):
    scale = 1.0 / (1024.0 * math.sqrt(ENERGIES))
    for w in range(0, b_ref.shape[-1], TILE):
        lanes = slice(w, w + TILE)
        re0, re1 = halves(b_ref, 0, lanes)
        im0, im1 = halves(b_ref, 1, lanes)
        low_re = low_im = high_re = high_im = None
        for r in range(4):
            re = (re0 + re1, re0 - im1, re0 - re1, re0 + im1)[r]
            im = (im0 + im1, im0 + re1, im0 - im1, im0 - re1)[r]
            if r:
                c, s = turned(turn, r, lanes)
                re, im = re * c - im * s, im * c + re * s
            cos_re, cos_im, sin_re, sin_im = product(matrix, re, im)
            b_re, b_im = cos_re - sin_im, cos_im + sin_re
            a_re, a_im = spectrum[r, 0, :, lanes], spectrum[r, 1, :, lanes]
            cos_re, cos_im, sin_re, sin_im = product(
                matrix, a_re * b_re - a_im * b_im, a_re * b_im + a_im * b_re
            )
            re, im = cos_re - sin_im, cos_im + sin_re
            if r:
                re, im = re * c - im * s, re * s + im * c
            if r == 0:
                low_re, low_im, high_re, high_im = re, im, re, im
            else:
                low_re, low_im = low_re + re, low_im + im
                if r == 1:
                    high_re, high_im = high_re - im, high_im + re
                elif r == 2:
                    high_re, high_im = high_re - re, high_im - im
                else:
                    high_re, high_im = high_re + im, high_im - re
        shape = (16, 16, TILE)
        out[:16, :16, lanes] = (low_im * scale).reshape(shape)
        out[16:, :16, lanes] = (high_im * scale).reshape(shape)
        out[:16, 16:, lanes] = (low_re * -scale).reshape(shape)
        out[16:, 16:, lanes] = (high_re * -scale).reshape(shape)


def correlate(matrix, turn, spectrum, b):
    width = b.shape[-1]
    return pl.pallas_call(
        correlate_kernel,
        in_specs=[VMEM] * 4,
        out_specs=VMEM,
        out_shape=jax.ShapeDtypeStruct((PARTS, 32, width), F32),
        compiler_params=params(),
        cost_estimate=cost(width * 2 * 4 * 512 * 768 * 4, width * 12288),
        name="correlate",
    )(matrix, turn, spectrum, b)


def scatter_rows(row_of, column, values, out, packed):
    per = values.shape[-1] // 128

    def batch(k, _):
        blocks = []
        for b in range(BATCH):
            block = k * BATCH + b
            w = b % per * 128
            group = (column[pl.ds(block, 1), :] >> 7) & 3
            data = values[block // per, :, w : w + 128]
            blocks.append(jnp.concatenate([jnp.where(group == g, data, 0.0) for g in range(4)], 0).T)
        for b in range(BATCH):
            packed[b * 128 : (b + 1) * 128, :] = blocks[b]
        for r in range(0, BATCH * 128, UNROLL):
            first = pl.multiple_of(k * (BATCH * 128) + r, UNROLL)
            rows = [row_of[first + u] for u in range(UNROLL)]
            for u in range(UNROLL):
                row = packed[r + u : r + u + 1, :]
                pltpu.store(out.at[pl.ds(rows[u], 1), :], row, mask=row != 0.0)
        return 0

    lax.fori_loop(0, PARTS * per // BATCH, batch, 0)


def scatter_first_kernel(row_of, column, values, out, packed, slots, sem):
    slots[...] = jnp.zeros_like(slots)
    scatter_rows(row_of, column, values, slots, packed)
    save = pltpu.make_async_copy(slots, out.at[0], sem)
    save.start()
    save.wait()


def scatter_last_kernel(row_of, column, values, before, out, packed, slots, earlier, staged, in_sem, out_sem):
    load = pltpu.make_async_copy(before.at[0], earlier, in_sem)
    load.start()
    slots[...] = jnp.zeros_like(slots)
    scatter_rows(row_of, column, values, slots, packed)
    load.wait()
    pieces = out_sem.shape[0]
    span = SLOTS // pieces
    copies = []
    for p in range(pieces):
        for q in range(p * span // 512, (p + 1) * span // 512):
            rows = slice(q * 128, (q + 1) * 128)
            block = (slots[rows, :] + earlier[rows, :]).T
            for g in range(4):
                s = slice(q * 512 + g * 128, q * 512 + (g + 1) * 128)
                staged[:, :, s] = block[g * 32 : (g + 1) * 32].reshape(2, 16, 128)
        piece = slice(p * span, (p + 1) * span)
        copies.append(pltpu.make_async_copy(staged.at[:, :, piece], out.at[:, :, piece], out_sem.at[p]))
        copies[-1].start()
    for copy in copies:
        copy.wait()


def scatter(columns, values, before):
    width = values.shape[-1]
    items = PARTS * width
    row_of = ((columns >> 9 << 7) | (columns & 127)).reshape(items)
    first = before is None
    scratch = [
        pltpu.VMEM((BATCH * 128, 128), F32),
        pltpu.VMEM((SLOTS // 4, 128), F32),
    ]
    if first:
        scratch += [pltpu.SemaphoreType.DMA]
    else:
        scratch += [
            pltpu.VMEM((SLOTS // 4, 128), F32),
            pltpu.VMEM((2, 16, SLOTS), F32),
            pltpu.SemaphoreType.DMA,
            pltpu.SemaphoreType.DMA((8,)),
        ]
    return pl.pallas_call(
        scatter_first_kernel if first else scatter_last_kernel,
        in_specs=[SMEM, VMEM, VMEM] + ([] if first else [ANY]),
        out_specs=ANY,
        out_shape=jax.ShapeDtypeStruct((6, SLOTS // 4, 128) if first else (2, 16, SLOTS), F32),
        scratch_shapes=scratch,
        compiler_params=params(44 << 20),
        cost_estimate=cost(items * 1000, items * 4000),
        name="scatter",
    )(row_of, columns, values, *(() if first else (before,)))


def local(g_lesser, g_greater, live_columns, live_count, mirror):
    slabs = lax.axis_size("slab")
    across = [(s, slabs - 1 - s) for s in range(slabs)]
    is_upper = lax.axis_index("slab") >= slabs // 2
    other_mirror = lax.ppermute(mirror, "slab", across)
    other_live = lax.ppermute(live_columns[:LIVE], "slab", across)
    order = jnp.where(is_upper, other_live, live_columns[:LIVE])
    table = jnp.where(is_upper, other_mirror, jnp.arange(SLOTS, dtype=jnp.int32))
    matrix, turn = tables()
    matrix, turn = jnp.asarray(matrix), jnp.asarray(turn)

    rows = column_rows(g_lesser, g_greater)
    half = WIDTHS[0]
    orders = [order[: PARTS * half], order[PARTS * half :]]
    picked0, columns0 = gather(live_count, orders[0], table, rows, 0, half)
    picked1, columns1 = gather(live_count, orders[1], table, rows, PARTS * half, WIDTHS[1])

    def swap(values):
        return lax.all_to_all(values, "energy", 0, 0, tiled=True)

    def mirrored(arrived):
        return lax.ppermute(arrived[:, 32:], "slab", across)

    arrived0 = swap(picked0)
    mirrored0 = mirrored(arrived0)
    arrived1 = swap(picked1)
    spectrum0 = lesser_spectrum(matrix, turn, arrived0)
    arrived1, spectrum0 = lax.optimization_barrier((arrived1, spectrum0))
    mirrored1 = mirrored(arrived1)
    polar0 = swap(correlate(matrix, turn, spectrum0, mirrored0))
    spectrum1 = lesser_spectrum(matrix, turn, arrived1)
    polar1 = swap(correlate(matrix, turn, spectrum1, mirrored1))
    slots = scatter(columns0, polar0, None)
    return scatter(columns1, polar1, slots)


def solution(mesh):
    spec = jax.P(None, "energy", "slab")
    return jax.shard_map(
        local,
        mesh=mesh,
        in_specs=(spec, spec, jax.P("slab"), jax.P("slab"), jax.P("slab")),
        out_specs=spec,
        check_vma=False,
    )
```

```python
import functools
import math

import jax
import jax.numpy as jnp
import ml_dtypes
import numpy as np
from jax import lax
from jax.experimental import pallas as pl
from jax.experimental.pallas import tpu as pltpu

F32 = jnp.float32
BF16 = jnp.bfloat16
SLOTS = 32768
LIVE = 16384
ENERGIES = 512
PARTS = 32
WIDTHS = (256, 256)
VMEM_BYTES = 60 << 20
SMEM = pl.BlockSpec(memory_space=pltpu.SMEM)
VMEM = pl.BlockSpec(memory_space=pltpu.VMEM)
ANY = pl.BlockSpec(memory_space=pl.ANY)
UNROLL = 32
BATCH = 4
TILE = 256


def params(limit=VMEM_BYTES):
    return pltpu.CompilerParams(vmem_limit_bytes=limit)


def cost(flops, bytes_accessed):
    return pl.CostEstimate(flops=flops, bytes_accessed=bytes_accessed, transcendentals=0)


def rows_kernel(a_low, b_low, a_high, b_high, rows):
    for j in range(a_low.shape[-1] // 128):
        s = slice(j * 128, (j + 1) * 128)
        block = [ref[:, :, s].reshape(32, 128) for ref in (a_low, b_low, a_high, b_high)]
        rows[s, :] = jnp.concatenate(block, 0).T


def column_rows(a, b, block=4096):
    steps = LIVE // block
    low = pl.BlockSpec((2, 16, block), lambda i: (0, 0, i))
    high = pl.BlockSpec((2, 16, block), lambda i: (0, 0, i + steps))
    return pl.pallas_call(
        rows_kernel,
        grid=(steps,),
        in_specs=[low, low, high, high],
        out_specs=pl.BlockSpec((block, 128), lambda i: (i, 0)),
        out_shape=jax.ShapeDtypeStruct((LIVE, 128), F32),
        compiler_params=params(),
        cost_estimate=cost(1 << 20, 24 << 20),
        name="column_rows",
    )(a, b, a, b)


def gather_kernel(count, upper, own, other, identity, mirror, rows, out, places, *rest, base):
    early, (packed, order, mapped, table, sems, row_sems) = rest[:-6], rest[-6:]
    width = out.shape[-1]
    per = width // 128
    here = pl.ds(base, PARTS * width)
    lists = [
        pltpu.make_async_copy(identity, mapped, sems.at[0]),
        pltpu.make_async_copy(own.at[here], order, sems.at[1]),
    ]
    other_lists = [
        pltpu.make_async_copy(mirror, mapped, sems.at[0]),
        pltpu.make_async_copy(other.at[here], order, sems.at[1]),
    ]

    @pl.when(upper[0] == 0)
    def _():
        for copy in lists:
            copy.start()

    @pl.when(upper[0] != 0)
    def _():
        for copy in other_lists:
            copy.start()

    parts = row_sems.shape[0]
    span = LIVE // parts
    loads = []
    for p in range(parts):
        s = pl.ds(p * span, span)
        loads.append(pltpu.make_async_copy(rows.at[s, :], table.at[s, :], row_sems.at[p]))
    for copy in loads:
        copy.start()
    step = 2048
    first_half = lax.broadcasted_iota(jnp.int32, (8, 128), 1) < 64
    number = lax.broadcasted_iota(jnp.int32, (8, 128), 0).astype(F32)
    for p in range(parts):
        loads[p].wait()

        def widen(k, _):
            first = pl.multiple_of(p * span + k * step, step)
            offset = number + first.astype(F32)
            for r in range(0, step, 8):
                both = table[pl.ds(first + r, 8), :]
                high = pltpu.roll(both, 64, 1)
                column = offset + float(r)
                table[pl.ds(first + r, 8), :] = jnp.where(first_half, both, column)
                table[pl.ds(first + r + LIVE, 8), :] = jnp.where(first_half, high, column + float(LIVE))
            return 0

        lax.fori_loop(0, span // step, widen, 0)
    for copy in lists:
        copy.wait()
    lane = lax.broadcasted_iota(jnp.int32, (1, 128), 1)

    def batch(k, _):
        for r in range(0, BATCH * 128, UNROLL):
            first = pl.multiple_of(k * (BATCH * 128) + r, UNROLL)
            cols = [mapped[order[first + u]] for u in range(UNROLL)]
            for u in range(UNROLL):
                packed[r + u : r + u + 1, :] = table[pl.ds(cols[u], 1), :]
        blocks = [packed[b * 128 : (b + 1) * 128, :].T for b in range(BATCH)]
        for b in range(BATCH):
            block = k * BATCH + b
            w = b % per * 128
            live = lane + (block * 128 + base) < count[0]
            values = jnp.where(live, blocks[b][:64], 0.0)
            out[block // per, :, w : w + 128] = values
            if early and w == 0:
                early[0][block // per] = values[32:]
            places[pl.ds(block, 1), :] = blocks[b][64:65].astype(jnp.int32)
        return 0

    lax.fori_loop(0, PARTS * per // BATCH, batch, 0)


def gather(lists, rows, base, width, early):
    items = PARTS * width
    return pl.pallas_call(
        functools.partial(gather_kernel, base=base),
        in_specs=[SMEM, SMEM, ANY, ANY, ANY, ANY, ANY],
        out_specs=[VMEM] * (3 if early else 2),
        out_shape=[
            jax.ShapeDtypeStruct((PARTS, 64, width), F32),
            jax.ShapeDtypeStruct((items // 128, 128), jnp.int32),
            jax.ShapeDtypeStruct((PARTS, 32, 128), F32),
        ][: 3 if early else 2],
        scratch_shapes=[
            pltpu.VMEM((BATCH * 128, 128), F32),
            pltpu.SMEM((items,), jnp.int32),
            pltpu.SMEM((SLOTS,), jnp.int32),
            pltpu.VMEM((SLOTS, 128), F32),
            pltpu.SemaphoreType.DMA((2,)),
            pltpu.SemaphoreType.DMA((4,)),
        ],
        compiler_params=params(),
        cost_estimate=cost(items * 2000, items * 5000),
        name="gather",
    )(*lists, rows)


def place_kernel(_, early, both, sem):
    copy = pltpu.make_async_copy(early, both.at[:, 32:, :128], sem)
    copy.start()
    copy.wait()


def place_early(both, early):
    return pl.pallas_call(
        place_kernel,
        in_specs=[ANY, ANY],
        out_specs=ANY,
        out_shape=jax.ShapeDtypeStruct(both.shape, F32),
        input_output_aliases={0: 0},
        scratch_shapes=[pltpu.SemaphoreType.DMA],
        compiler_params=params(),
        cost_estimate=cost(1 << 20, 2 << 20),
        name="place_early",
    )(both, early)


def tables():
    n = np.arange(256)
    angle = 2.0 * np.pi * ((n[:, None] * n[None, :]) % 256) / 256.0
    matrix = np.concatenate([np.cos(angle), np.sin(angle)], 0).astype(np.float32)
    high = matrix.astype(ml_dtypes.bfloat16)
    low = (matrix - high.astype(np.float32)).astype(ml_dtypes.bfloat16)
    matrix = np.concatenate([high, high, low], 1)
    phase = 2.0 * np.pi * np.arange(1, 4)[:, None] * n[None, :] / 1024.0
    turn = np.stack([np.cos(phase), np.sin(phase)], 1).astype(np.float32)
    return matrix, np.repeat(turn[:, :, :, None], 128, 3)


def split(values):
    high = values.astype(BF16)
    low = (values - high.astype(F32)).astype(BF16)
    return jnp.concatenate([high, low, high], 0)


def halves(ref, part, lanes):
    values = ref[:, part * 16 : part * 16 + 16, lanes].reshape(ENERGIES, -1)
    return values[:256], values[256:]


def turned(turn, r, lanes):
    repeat = (lanes.stop - lanes.start) // 128
    return [jnp.concatenate([turn[r - 1, part]] * repeat, 1) for part in range(2)]


def product(matrix, re, im):
    both = jnp.dot(matrix[...], split(jnp.concatenate([re, im], 1)), preferred_element_type=F32)
    half = re.shape[1]
    return both[:256, :half], both[:256, half:], both[256:, :half], both[256:, half:]


def lesser_kernel(matrix, turn, both_in, spectrum, both, sem):
    load = pltpu.make_async_copy(both_in.at[:, :32, :], both, sem)
    load.start()
    load.wait()
    tile = min(TILE, both.shape[-1])
    for w in range(0, both.shape[-1], tile):
        lanes = slice(w, w + tile)
        re0, re1 = halves(both, 0, lanes)
        im0, im1 = halves(both, 1, lanes)
        for r in range(4):
            re = (re0 + re1, re0 + im1, re0 - re1, re0 - im1)[r]
            im = (im0 + im1, im0 - re1, im0 - im1, im0 + re1)[r]
            if r:
                c, s = turned(turn, r, lanes)
                re, im = re * c + im * s, im * c - re * s
            cos_re, cos_im, sin_re, sin_im = product(matrix, re, im)
            spectrum[r, 0, :, lanes] = cos_re + sin_im
            spectrum[r, 1, :, lanes] = cos_im - sin_re


def lesser_spectrum(matrix, turn, both):
    width = both.shape[-1]
    return pl.pallas_call(
        lesser_kernel,
        in_specs=[VMEM, VMEM, ANY],
        out_specs=VMEM,
        out_shape=jax.ShapeDtypeStruct((4, 2, 256, width), F32),
        scratch_shapes=[pltpu.VMEM((PARTS, 32, width), F32), pltpu.SemaphoreType.DMA],
        compiler_params=params(),
        cost_estimate=cost(width * 2 * 4 * 512 * 768 * 2, width * 12288),
        name="lesser_spectrum",
    )(matrix, turn, both)


def correlate_kernel(matrix_in, turn_in, spectrum_in, b_in, *rest, lanes):
    result, matrix, turn, spectrum, b_ref, out, sems = rest[-7:]
    b_lanes = slice(None) if b_in.shape[-1] == out.shape[-1] else lanes
    loads = [
        pltpu.make_async_copy(b_in.at[:, b_in.shape[1] - 32 :, b_lanes], b_ref, sems.at[0]),
        pltpu.make_async_copy(matrix_in, matrix, sems.at[1]),
        pltpu.make_async_copy(spectrum_in.at[:, :, :, lanes], spectrum, sems.at[2]),
        pltpu.make_async_copy(turn_in, turn, sems.at[3]),
    ]
    for load in loads:
        load.start()
    for load in loads:
        load.wait()
    scale = 1.0 / (1024.0 * math.sqrt(ENERGIES))
    tile = min(TILE, out.shape[-1])
    for w in range(0, out.shape[-1], tile):
        part = slice(w, w + tile)
        re0, re1 = halves(b_ref, 0, part)
        im0, im1 = halves(b_ref, 1, part)
        low_re = low_im = high_re = high_im = None
        for r in range(4):
            re = (re0 + re1, re0 - im1, re0 - re1, re0 + im1)[r]
            im = (im0 + im1, im0 + re1, im0 - im1, im0 - re1)[r]
            if r:
                c, s = turned(turn, r, part)
                re, im = re * c - im * s, im * c + re * s
            cos_re, cos_im, sin_re, sin_im = product(matrix, re, im)
            b_re, b_im = cos_re - sin_im, cos_im + sin_re
            a_re, a_im = spectrum[r, 0, :, part], spectrum[r, 1, :, part]
            cos_re, cos_im, sin_re, sin_im = product(
                matrix, a_re * b_re - a_im * b_im, a_re * b_im + a_im * b_re
            )
            re, im = cos_re - sin_im, cos_im + sin_re
            if r:
                re, im = re * c - im * s, re * s + im * c
            if r == 0:
                low_re, low_im, high_re, high_im = re, im, re, im
            else:
                low_re, low_im = low_re + re, low_im + im
                if r == 1:
                    high_re, high_im = high_re - im, high_im + re
                elif r == 2:
                    high_re, high_im = high_re - re, high_im - im
                else:
                    high_re, high_im = high_re + im, high_im - re
        shape = (16, 16, tile)
        out[:16, :16, part] = (low_im * scale).reshape(shape)
        out[16:, :16, part] = (high_im * scale).reshape(shape)
        out[:16, 16:, part] = (low_re * -scale).reshape(shape)
        out[16:, 16:, part] = (high_re * -scale).reshape(shape)
    save = pltpu.make_async_copy(out, result.at[:, :, lanes], sems.at[0])
    save.start()
    save.wait()


def correlate(matrix, turn, spectrum, b, lanes, into=None):
    width = spectrum.shape[-1]
    part = lanes.stop - lanes.start
    more = () if into is None else (into,)
    return pl.pallas_call(
        functools.partial(correlate_kernel, lanes=lanes),
        in_specs=[ANY] * (4 + len(more)),
        out_specs=ANY,
        out_shape=jax.ShapeDtypeStruct((PARTS, 32, width), F32),
        input_output_aliases={4: 0} if more else {},
        scratch_shapes=[
            pltpu.VMEM(matrix.shape, BF16),
            pltpu.VMEM(turn.shape, F32),
            pltpu.VMEM((4, 2, 256, part), F32),
            pltpu.VMEM((PARTS, 32, part), F32),
            pltpu.VMEM((PARTS, 32, part), F32),
            pltpu.SemaphoreType.DMA((4,)),
        ],
        compiler_params=params(),
        cost_estimate=cost(part * 2 * 4 * 512 * 768 * 4, part * 12288),
        name="correlate",
    )(matrix, turn, spectrum, b, *more)


def scatter_rows(row_of, column, values, out, packed):
    per = values.shape[-1] // 128

    def batch(k, _):
        blocks = []
        for b in range(BATCH):
            block = k * BATCH + b
            w = b % per * 128
            group = (column[pl.ds(block, 1), :] >> 7) & 3
            data = values[block // per, :, w : w + 128]
            blocks.append(jnp.concatenate([jnp.where(group == g, data, 0.0) for g in range(4)], 0).T)
        for b in range(BATCH):
            packed[b * 128 : (b + 1) * 128, :] = blocks[b]
        for r in range(0, BATCH * 128, UNROLL):
            first = pl.multiple_of(k * (BATCH * 128) + r, UNROLL)
            rows = [row_of[first + u] for u in range(UNROLL)]
            for u in range(UNROLL):
                row = packed[r + u : r + u + 1, :]
                pltpu.store(out.at[pl.ds(rows[u], 1), :], row, mask=row != 0.0)
        return 0

    lax.fori_loop(0, PARTS * per // BATCH, batch, 0)


def scatter_first_kernel(row_of, column, values, out, packed, slots, sem):
    slots[...] = jnp.zeros_like(slots)
    scatter_rows(row_of, column, values, slots, packed)
    save = pltpu.make_async_copy(slots, out.at[0], sem)
    save.start()
    save.wait()


def scatter_last_kernel(row_of, column, values, before, out, packed, slots, earlier, staged, in_sem, out_sem):
    load = pltpu.make_async_copy(before.at[0], earlier, in_sem)
    load.start()
    slots[...] = jnp.zeros_like(slots)
    scatter_rows(row_of, column, values, slots, packed)
    load.wait()
    pieces = out_sem.shape[0]
    span = SLOTS // pieces
    copies = []
    for p in range(pieces):
        for q in range(p * span // 512, (p + 1) * span // 512):
            rows = slice(q * 128, (q + 1) * 128)
            block = (slots[rows, :] + earlier[rows, :]).T
            for g in range(4):
                s = slice(q * 512 + g * 128, q * 512 + (g + 1) * 128)
                staged[:, :, s] = block[g * 32 : (g + 1) * 32].reshape(2, 16, 128)
        piece = slice(p * span, (p + 1) * span)
        copies.append(pltpu.make_async_copy(staged.at[:, :, piece], out.at[:, :, piece], out_sem.at[p]))
        copies[-1].start()
    for copy in copies:
        copy.wait()


def scatter(columns, values, before):
    width = values.shape[-1]
    items = PARTS * width
    row_of = ((columns >> 9 << 7) | (columns & 127)).reshape(items)
    first = before is None
    scratch = [
        pltpu.VMEM((BATCH * 128, 128), F32),
        pltpu.VMEM((SLOTS // 4, 128), F32),
    ]
    if first:
        scratch += [pltpu.SemaphoreType.DMA]
    else:
        scratch += [
            pltpu.VMEM((SLOTS // 4, 128), F32),
            pltpu.VMEM((2, 16, SLOTS), F32),
            pltpu.SemaphoreType.DMA,
            pltpu.SemaphoreType.DMA((8,)),
        ]
    return pl.pallas_call(
        scatter_first_kernel if first else scatter_last_kernel,
        in_specs=[SMEM, VMEM, VMEM] + ([] if first else [ANY]),
        out_specs=ANY,
        out_shape=jax.ShapeDtypeStruct((6, SLOTS // 4, 128) if first else (2, 16, SLOTS), F32),
        scratch_shapes=scratch,
        compiler_params=params(44 << 20),
        cost_estimate=cost(items * 1000, items * 4000),
        name="scatter",
    )(row_of, columns, values, *(() if first else (before,)))


def local(g_lesser, g_greater, live_columns, live_count, mirror):
    slabs = lax.axis_size("slab")
    across = [(s, slabs - 1 - s) for s in range(slabs)]
    upper = (lax.axis_index("slab") >= slabs // 2).astype(jnp.int32).reshape(1)
    other_mirror = lax.ppermute(mirror, "slab", across)
    other_live = lax.ppermute(live_columns, "slab", across)
    identity = jnp.asarray(np.arange(SLOTS, dtype=np.int32))
    lists = (live_count, upper, live_columns, other_live, identity, other_mirror)
    matrix, turn = tables()
    matrix, turn = jnp.asarray(matrix), jnp.asarray(turn)
    first, second = slice(0, 128), slice(128, 256)

    def swap(values):
        return lax.all_to_all(values, "energy", 0, 0, tiled=True)

    def cross(values):
        return lax.ppermute(values, "slab", across)

    rows = column_rows(g_lesser, g_greater)
    picked0, columns0 = gather(lists, rows, 0, WIDTHS[0], False)
    picked1, columns1, early = gather(lists, rows, PARTS * WIDTHS[0], WIDTHS[1], True)
    early = cross(early)
    arrived0 = swap(picked0)
    lesser0, greater0 = arrived0[:, :32], arrived0[:, 32:]
    early, greater0 = lax.optimization_barrier((early, greater0))
    mirrored0 = cross(greater0)
    arrived1 = swap(place_early(picked1, early))
    spectrum0 = lesser_spectrum(matrix, turn, lesser0)
    result0 = correlate(matrix, turn, spectrum0, mirrored0, slice(0, 256))
    arrived1, result0 = lax.optimization_barrier((arrived1, result0))
    mirrored1 = cross(arrived1[:, 32:, second])
    polar0 = swap(result0)
    spectrum1 = lesser_spectrum(matrix, turn, arrived1)
    result1 = correlate(matrix, turn, spectrum1, arrived1, first)
    polar1 = swap(correlate(matrix, turn, spectrum1, mirrored1, second, result1))
    slots = scatter(columns0, polar0, None)
    return scatter(columns1, polar1, slots)


def solution(mesh):
    spec = jax.P(None, "energy", "slab")
    return jax.shard_map(
        local,
        mesh=mesh,
        in_specs=(spec, spec, jax.P("slab"), jax.P("slab"), jax.P("slab")),
        out_specs=spec,
        check_vma=False,
    )
```

```python
import functools
import math

import jax
import jax.numpy as jnp
import ml_dtypes
import numpy as np
from jax import lax
from jax.experimental import pallas as pl
from jax.experimental.pallas import tpu as pltpu

F32 = jnp.float32
BF16 = jnp.bfloat16
SLOTS = 32768
LIVE = 16384
ENERGIES = 512
PARTS = 32
WIDTHS = (256, 256)
VMEM_BYTES = 60 << 20
SMEM = pl.BlockSpec(memory_space=pltpu.SMEM)
VMEM = pl.BlockSpec(memory_space=pltpu.VMEM)
ANY = pl.BlockSpec(memory_space=pl.ANY)
UNROLL = 32
BATCH = 4
TILE = 256


def params(limit=VMEM_BYTES):
    return pltpu.CompilerParams(vmem_limit_bytes=limit)


def cost(flops, bytes_accessed):
    return pl.CostEstimate(flops=flops, bytes_accessed=bytes_accessed, transcendentals=0)


def rows_kernel(a_low, b_low, a_high, b_high, rows):
    for j in range(a_low.shape[-1] // 128):
        s = slice(j * 128, (j + 1) * 128)
        block = [ref[:, :, s].reshape(32, 128) for ref in (a_low, b_low, a_high, b_high)]
        rows[s, :] = jnp.concatenate(block, 0).T


def column_rows(a, b, block=4096):
    steps = LIVE // block
    low = pl.BlockSpec((2, 16, block), lambda i: (0, 0, i))
    high = pl.BlockSpec((2, 16, block), lambda i: (0, 0, i + steps))
    return pl.pallas_call(
        rows_kernel,
        grid=(steps,),
        in_specs=[low, low, high, high],
        out_specs=pl.BlockSpec((block, 128), lambda i: (i, 0)),
        out_shape=jax.ShapeDtypeStruct((LIVE, 128), F32),
        compiler_params=params(),
        cost_estimate=cost(1 << 20, 24 << 20),
        name="column_rows",
    )(a, b, a, b)


def gather_kernel(
    count, upper, own, other, identity, mirror, rows, out, places, packed, order, mapped, table, sems, row_sems, *, base
):
    width = out.shape[-1]
    per = width // 128
    here = pl.ds(base, PARTS * width)
    lists = [
        pltpu.make_async_copy(identity, mapped, sems.at[0]),
        pltpu.make_async_copy(own.at[here], order, sems.at[1]),
    ]
    other_lists = [
        pltpu.make_async_copy(mirror, mapped, sems.at[0]),
        pltpu.make_async_copy(other.at[here], order, sems.at[1]),
    ]

    @pl.when(upper[0] == 0)
    def _():
        for copy in lists:
            copy.start()

    @pl.when(upper[0] != 0)
    def _():
        for copy in other_lists:
            copy.start()

    parts = row_sems.shape[0]
    span = LIVE // parts
    loads = []
    for p in range(parts):
        s = pl.ds(p * span, span)
        loads.append(pltpu.make_async_copy(rows.at[s, :], table.at[s, :], row_sems.at[p]))
    for copy in loads:
        copy.start()
    step = 2048
    first_half = lax.broadcasted_iota(jnp.int32, (8, 128), 1) < 64
    number = lax.broadcasted_iota(jnp.int32, (8, 128), 0).astype(F32)
    for p in range(parts):
        loads[p].wait()

        def widen(k, _):
            first = pl.multiple_of(p * span + k * step, step)
            offset = number + first.astype(F32)
            for r in range(0, step, 8):
                both = table[pl.ds(first + r, 8), :]
                high = pltpu.roll(both, 64, 1)
                column = offset + float(r)
                table[pl.ds(first + r, 8), :] = jnp.where(first_half, both, column)
                table[pl.ds(first + r + LIVE, 8), :] = jnp.where(first_half, high, column + float(LIVE))
            return 0

        lax.fori_loop(0, span // step, widen, 0)
    for copy in lists:
        copy.wait()
    lane = lax.broadcasted_iota(jnp.int32, (1, 128), 1)

    def batch(k, _):
        for r in range(0, BATCH * 128, UNROLL):
            first = pl.multiple_of(k * (BATCH * 128) + r, UNROLL)
            cols = [mapped[order[first + u]] for u in range(UNROLL)]
            for u in range(UNROLL):
                packed[r + u : r + u + 1, :] = table[pl.ds(cols[u], 1), :]
        blocks = [packed[b * 128 : (b + 1) * 128, :].T for b in range(BATCH)]
        for b in range(BATCH):
            block = k * BATCH + b
            w = b % per * 128
            live = lane + (block * 128 + base) < count[0]
            out[block // per, :, w : w + 128] = jnp.where(live, blocks[b][:64], 0.0)
            places[pl.ds(block, 1), :] = blocks[b][64:65].astype(jnp.int32)
        return 0

    lax.fori_loop(0, PARTS * per // BATCH, batch, 0)


def gather(lists, rows, base, width):
    items = PARTS * width
    return pl.pallas_call(
        functools.partial(gather_kernel, base=base),
        in_specs=[SMEM, SMEM, ANY, ANY, ANY, ANY, ANY],
        out_specs=[VMEM, VMEM],
        out_shape=[
            jax.ShapeDtypeStruct((PARTS, 64, width), F32),
            jax.ShapeDtypeStruct((items // 128, 128), jnp.int32),
        ],
        scratch_shapes=[
            pltpu.VMEM((BATCH * 128, 128), F32),
            pltpu.SMEM((items,), jnp.int32),
            pltpu.SMEM((SLOTS,), jnp.int32),
            pltpu.VMEM((SLOTS, 128), F32),
            pltpu.SemaphoreType.DMA((2,)),
            pltpu.SemaphoreType.DMA((4,)),
        ],
        compiler_params=params(),
        cost_estimate=cost(items * 2000, items * 5000),
        name="gather",
    )(*lists, rows)


def tables():
    n = np.arange(256)
    angle = 2.0 * np.pi * ((n[:, None] * n[None, :]) % 256) / 256.0
    matrix = np.concatenate([np.cos(angle), np.sin(angle)], 0).astype(np.float32)
    high = matrix.astype(ml_dtypes.bfloat16)
    low = (matrix - high.astype(np.float32)).astype(ml_dtypes.bfloat16)
    matrix = np.concatenate([high, high, low], 1)
    phase = 2.0 * np.pi * np.arange(1, 4)[:, None] * n[None, :] / 1024.0
    turn = np.stack([np.cos(phase), np.sin(phase)], 1).astype(np.float32)
    return matrix, np.repeat(turn[:, :, :, None], 128, 3)


def split(values):
    high = values.astype(BF16)
    low = (values - high.astype(F32)).astype(BF16)
    return jnp.concatenate([high, low, high], 0)


def halves(ref, part, lanes):
    values = ref[:, part * 16 : part * 16 + 16, lanes].reshape(ENERGIES, -1)
    return values[:256], values[256:]


def turned(turn, r, lanes):
    repeat = (lanes.stop - lanes.start) // 128
    return [jnp.concatenate([turn[r - 1, part]] * repeat, 1) for part in range(2)]


def product(matrix, re, im):
    both = jnp.dot(matrix[...], split(jnp.concatenate([re, im], 1)), preferred_element_type=F32)
    half = re.shape[1]
    return both[:256, :half], both[:256, half:], both[256:, :half], both[256:, half:]


def lesser_kernel(matrix, turn, both_in, spectrum, both, sem):
    load = pltpu.make_async_copy(both_in.at[:, :32, :], both, sem)
    load.start()
    load.wait()
    tile = min(TILE, both.shape[-1])
    for w in range(0, both.shape[-1], tile):
        lanes = slice(w, w + tile)
        re0, re1 = halves(both, 0, lanes)
        im0, im1 = halves(both, 1, lanes)
        for r in range(4):
            re = (re0 + re1, re0 + im1, re0 - re1, re0 - im1)[r]
            im = (im0 + im1, im0 - re1, im0 - im1, im0 + re1)[r]
            if r:
                c, s = turned(turn, r, lanes)
                re, im = re * c + im * s, im * c - re * s
            cos_re, cos_im, sin_re, sin_im = product(matrix, re, im)
            spectrum[r, 0, :, lanes] = cos_re + sin_im
            spectrum[r, 1, :, lanes] = cos_im - sin_re


def lesser_spectrum(matrix, turn, both):
    width = both.shape[-1]
    return pl.pallas_call(
        lesser_kernel,
        in_specs=[VMEM, VMEM, ANY],
        out_specs=VMEM,
        out_shape=jax.ShapeDtypeStruct((4, 2, 256, width), F32),
        scratch_shapes=[pltpu.VMEM((PARTS, 32, width), F32), pltpu.SemaphoreType.DMA],
        compiler_params=params(),
        cost_estimate=cost(width * 2 * 4 * 512 * 768 * 2, width * 12288),
        name="lesser_spectrum",
    )(matrix, turn, both)


def correlate_kernel(matrix_in, turn_in, spectrum_in, b_in, out, matrix, turn, spectrum, b_ref, sems):
    loads = [
        pltpu.make_async_copy(b_in, b_ref, sems.at[0]),
        pltpu.make_async_copy(matrix_in, matrix, sems.at[1]),
        pltpu.make_async_copy(spectrum_in, spectrum, sems.at[2]),
        pltpu.make_async_copy(turn_in, turn, sems.at[3]),
    ]
    for load in loads:
        load.start()
    loads[0].wait()
    loads[1].wait()
    scale = 1.0 / (1024.0 * math.sqrt(ENERGIES))
    tile = min(TILE, out.shape[-1])
    for w in range(0, out.shape[-1], tile):
        part = slice(w, w + tile)
        re0, re1 = halves(b_ref, 0, part)
        im0, im1 = halves(b_ref, 1, part)
        low_re = low_im = high_re = high_im = None
        for r in range(4):
            re = (re0 + re1, re0 - im1, re0 - re1, re0 + im1)[r]
            im = (im0 + im1, im0 + re1, im0 - im1, im0 - re1)[r]
            if r:
                if w == 0 and r == 1:
                    loads[3].wait()
                c, s = turned(turn, r, part)
                re, im = re * c - im * s, im * c + re * s
            cos_re, cos_im, sin_re, sin_im = product(matrix, re, im)
            b_re, b_im = cos_re - sin_im, cos_im + sin_re
            if w == 0 and r == 0:
                loads[2].wait()
            a_re, a_im = spectrum[r, 0, :, part], spectrum[r, 1, :, part]
            cos_re, cos_im, sin_re, sin_im = product(
                matrix, a_re * b_re - a_im * b_im, a_re * b_im + a_im * b_re
            )
            re, im = cos_re - sin_im, cos_im + sin_re
            if r:
                re, im = re * c - im * s, re * s + im * c
            if r == 0:
                low_re, low_im, high_re, high_im = re, im, re, im
            else:
                low_re, low_im = low_re + re, low_im + im
                if r == 1:
                    high_re, high_im = high_re - im, high_im + re
                elif r == 2:
                    high_re, high_im = high_re - re, high_im - im
                else:
                    high_re, high_im = high_re + im, high_im - re
        shape = (16, 16, tile)
        out[:16, :16, part] = (low_im * scale).reshape(shape)
        out[16:, :16, part] = (high_im * scale).reshape(shape)
        out[:16, 16:, part] = (low_re * -scale).reshape(shape)
        out[16:, 16:, part] = (high_re * -scale).reshape(shape)


def correlate(matrix, turn, spectrum, b):
    width = b.shape[-1]
    return pl.pallas_call(
        correlate_kernel,
        in_specs=[ANY] * 4,
        out_specs=VMEM,
        out_shape=jax.ShapeDtypeStruct((PARTS, 32, width), F32),
        scratch_shapes=[
            pltpu.VMEM(matrix.shape, BF16),
            pltpu.VMEM(turn.shape, F32),
            pltpu.VMEM(spectrum.shape, F32),
            pltpu.VMEM(b.shape, F32),
            pltpu.SemaphoreType.DMA((4,)),
        ],
        compiler_params=params(),
        cost_estimate=cost(width * 2 * 4 * 512 * 768 * 4, width * 12288),
        name="correlate",
    )(matrix, turn, spectrum, b)


def scatter_rows(row_of, column, values, out, packed):
    per = values.shape[-1] // 128

    def batch(k, _):
        blocks = []
        for b in range(BATCH):
            block = k * BATCH + b
            w = b % per * 128
            group = (column[pl.ds(block, 1), :] >> 7) & 3
            data = values[block // per, :, w : w + 128]
            blocks.append(jnp.concatenate([jnp.where(group == g, data, 0.0) for g in range(4)], 0).T)
        for b in range(BATCH):
            packed[b * 128 : (b + 1) * 128, :] = blocks[b]
        for r in range(0, BATCH * 128, UNROLL):
            first = pl.multiple_of(k * (BATCH * 128) + r, UNROLL)
            rows = [row_of[first + u] for u in range(UNROLL)]
            for u in range(UNROLL):
                row = packed[r + u : r + u + 1, :]
                pltpu.store(out.at[pl.ds(rows[u], 1), :], row, mask=row != 0.0)
        return 0

    lax.fori_loop(0, PARTS * per // BATCH, batch, 0)


def scatter_first_kernel(row_of, column, values, out, packed, slots, sem):
    slots[...] = jnp.zeros_like(slots)
    scatter_rows(row_of, column, values, slots, packed)
    save = pltpu.make_async_copy(slots, out.at[0], sem)
    save.start()
    save.wait()


def scatter_last_kernel(row_of, column, values, before, out, packed, slots, earlier, staged, in_sem, out_sem):
    load = pltpu.make_async_copy(before.at[0], earlier, in_sem)
    load.start()
    slots[...] = jnp.zeros_like(slots)
    scatter_rows(row_of, column, values, slots, packed)
    load.wait()
    pieces = out_sem.shape[0]
    span = SLOTS // pieces
    copies = []
    for p in range(pieces):
        for q in range(p * span // 512, (p + 1) * span // 512):
            rows = slice(q * 128, (q + 1) * 128)
            block = (slots[rows, :] + earlier[rows, :]).T
            for g in range(4):
                s = slice(q * 512 + g * 128, q * 512 + (g + 1) * 128)
                staged[:, :, s] = block[g * 32 : (g + 1) * 32].reshape(2, 16, 128)
        piece = slice(p * span, (p + 1) * span)
        copies.append(pltpu.make_async_copy(staged.at[:, :, piece], out.at[:, :, piece], out_sem.at[p]))
        copies[-1].start()
    for copy in copies:
        copy.wait()


def scatter(columns, values, before):
    width = values.shape[-1]
    items = PARTS * width
    row_of = ((columns >> 9 << 7) | (columns & 127)).reshape(items)
    first = before is None
    scratch = [
        pltpu.VMEM((BATCH * 128, 128), F32),
        pltpu.VMEM((SLOTS // 4, 128), F32),
    ]
    if first:
        scratch += [pltpu.SemaphoreType.DMA]
    else:
        scratch += [
            pltpu.VMEM((SLOTS // 4, 128), F32),
            pltpu.VMEM((2, 16, SLOTS), F32),
            pltpu.SemaphoreType.DMA,
            pltpu.SemaphoreType.DMA((8,)),
        ]
    return pl.pallas_call(
        scatter_first_kernel if first else scatter_last_kernel,
        in_specs=[SMEM, VMEM, VMEM] + ([] if first else [ANY]),
        out_specs=ANY,
        out_shape=jax.ShapeDtypeStruct((6, SLOTS // 4, 128) if first else (2, 16, SLOTS), F32),
        scratch_shapes=scratch,
        compiler_params=params(44 << 20),
        cost_estimate=cost(items * 1000, items * 4000),
        name="scatter",
    )(row_of, columns, values, *(() if first else (before,)))


def local(g_lesser, g_greater, live_columns, live_count, mirror):
    slabs = lax.axis_size("slab")
    across = [(s, slabs - 1 - s) for s in range(slabs)]
    upper = (lax.axis_index("slab") >= slabs // 2).astype(jnp.int32).reshape(1)
    other_mirror = lax.ppermute(mirror, "slab", across)
    other_live = lax.ppermute(live_columns, "slab", across)
    identity = jnp.asarray(np.arange(SLOTS, dtype=np.int32))
    lists = (live_count, upper, live_columns, other_live, identity, other_mirror)
    matrix, turn = tables()
    matrix, turn = jnp.asarray(matrix), jnp.asarray(turn)

    def swap(values):
        return lax.all_to_all(values, "energy", 0, 0, tiled=True)

    def cross(values):
        return lax.ppermute(values, "slab", across)

    rows = column_rows(g_lesser, g_greater)
    picked0, columns0 = gather(lists, rows, 0, WIDTHS[0])
    picked1, columns1 = gather(lists, rows, PARTS * WIDTHS[0], WIDTHS[1])
    arrived0 = swap(picked0)
    lesser0, greater0 = arrived0[:, :32], arrived0[:, 32:]
    mirrored0 = cross(greater0)
    arrived1 = swap(picked1)
    spectrum0 = lesser_spectrum(matrix, turn, lesser0)
    arrived1, spectrum0 = lax.optimization_barrier((arrived1, spectrum0))
    mirrored1 = cross(arrived1[:, 32:])
    polar0 = swap(correlate(matrix, turn, spectrum0, mirrored0))
    spectrum1 = lesser_spectrum(matrix, turn, arrived1)
    polar1 = swap(correlate(matrix, turn, spectrum1, mirrored1))
    slots = scatter(columns0, polar0, None)
    return scatter(columns1, polar1, slots)


def solution(mesh):
    spec = jax.P(None, "energy", "slab")
    return jax.shard_map(
        local,
        mesh=mesh,
        in_specs=(spec, spec, jax.P("slab"), jax.P("slab"), jax.P("slab")),
        out_specs=spec,
        check_vma=False,
    )
```

```python
import functools
import math

import jax
import jax.numpy as jnp
import ml_dtypes
import numpy as np
from jax import lax
from jax.experimental import pallas as pl
from jax.experimental.pallas import tpu as pltpu

F32 = jnp.float32
BF16 = jnp.bfloat16
SLOTS = 32768
LIVE = 16384
ENERGIES = 512
PARTS = 32
WIDTHS = (256, 256)
VMEM_BYTES = 60 << 20
SMEM = pl.BlockSpec(memory_space=pltpu.SMEM)
VMEM = pl.BlockSpec(memory_space=pltpu.VMEM)
ANY = pl.BlockSpec(memory_space=pl.ANY)
UNROLL = 32
BATCH = 8
TILE = 256


def params(limit=VMEM_BYTES):
    return pltpu.CompilerParams(vmem_limit_bytes=limit)


def cost(flops, bytes_accessed):
    return pl.CostEstimate(flops=flops, bytes_accessed=bytes_accessed, transcendentals=0)


def rows_kernel(a_low, b_low, a_high, b_high, rows, numbers):
    number = lax.broadcasted_iota(jnp.int32, numbers.shape, 0) * 128
    numbers[...] = number + lax.broadcasted_iota(jnp.int32, numbers.shape, 1)
    for j in range(a_low.shape[-1] // 128):
        s = slice(j * 128, (j + 1) * 128)
        block = [ref[:, :, s].reshape(32, 128) for ref in (a_low, b_low, a_high, b_high)]
        rows[s, :] = jnp.concatenate(block, 0).T


def column_rows(a, b, block=4096):
    steps = LIVE // block
    low = pl.BlockSpec((2, 16, block), lambda i: (0, 0, i))
    high = pl.BlockSpec((2, 16, block), lambda i: (0, 0, i + steps))
    return pl.pallas_call(
        rows_kernel,
        grid=(steps,),
        in_specs=[low, low, high, high],
        out_specs=[
            pl.BlockSpec((block, 128), lambda i: (i, 0)),
            pl.BlockSpec((SLOTS // 128, 128), lambda i: (0, 0)),
        ],
        out_shape=[
            jax.ShapeDtypeStruct((LIVE, 128), F32),
            jax.ShapeDtypeStruct((SLOTS // 128, 128), jnp.int32),
        ],
        compiler_params=params(),
        cost_estimate=cost(1 << 20, 24 << 20),
        name="column_rows",
    )(a, b, a, b)


def gather_kernel(
    count, upper, own, other, identity, mirror, rows, out, places,
    packed, list0, list1, mapped, table, map_sem, list_sems, row_sems, *, base
):
    width = out.shape[-1]
    per = width // 128
    lists = (list0, list1)
    items = BATCH * 128
    count_batches = PARTS * per // BATCH

    def fetch(source, batch, h):
        piece = pl.ds(pl.multiple_of(base + batch * items, items), items)
        return pltpu.make_async_copy(source.at[piece], lists[h], list_sems.at[h])

    def start(batch, h):
        @pl.when(upper[0] == 0)
        def _():
            fetch(own, batch, h).start()

        @pl.when(upper[0] != 0)
        def _():
            fetch(other, batch, h).start()

    @pl.when(upper[0] == 0)
    def _():
        pltpu.make_async_copy(identity, mapped, map_sem).start()

    @pl.when(upper[0] != 0)
    def _():
        pltpu.make_async_copy(mirror, mapped, map_sem).start()

    start(0, 0)
    start(1, 1)
    parts = row_sems.shape[0]
    span = LIVE // parts
    loads = []
    for p in range(parts):
        s = pl.ds(p * span, span)
        loads.append(pltpu.make_async_copy(rows.at[s, :], table.at[s, :], row_sems.at[p]))
    for copy in loads:
        copy.start()
    step = 2048
    first_half = lax.broadcasted_iota(jnp.int32, (8, 128), 1) < 64
    number = lax.broadcasted_iota(jnp.int32, (8, 128), 0).astype(F32)
    for p in range(parts):
        loads[p].wait()

        def widen(k, _):
            first = pl.multiple_of(p * span + k * step, step)
            offset = number + first.astype(F32)
            for r in range(0, step, 8):
                both = table[pl.ds(first + r, 8), :]
                high = pltpu.roll(both, 64, 1)
                column = offset + float(r)
                table[pl.ds(first + r, 8), :] = jnp.where(first_half, both, column)
                table[pl.ds(first + r + LIVE, 8), :] = jnp.where(first_half, high, column + float(LIVE))
            return 0

        lax.fori_loop(0, span // step, widen, 0)
    pltpu.make_async_copy(identity, mapped, map_sem).wait()
    lane = lax.broadcasted_iota(jnp.int32, (1, 128), 1)

    def pair(k, _):
        for h in range(2):
            batch = 2 * k + h
            fetch(own, batch, h).wait()
            for r in range(0, items, UNROLL):
                cols = [mapped[lists[h][r + u]] for u in range(UNROLL)]
                for u in range(UNROLL):
                    packed[r + u : r + u + 1, :] = table[pl.ds(cols[u], 1), :]

            @pl.when(batch + 2 < count_batches)
            def _():
                start(batch + 2, h)

            blocks = [packed[b * 128 : (b + 1) * 128, :].T for b in range(BATCH)]
            for b in range(BATCH):
                block = batch * BATCH + b
                w = b % per * 128
                live = lane + (block * 128 + base) < count[0]
                out[block // per, :, w : w + 128] = jnp.where(live, blocks[b][:64], 0.0)
                places[pl.ds(block, 1), :] = blocks[b][64:65].astype(jnp.int32)
        return 0

    lax.fori_loop(0, count_batches // 2, pair, 0)


def gather(lists, rows, base, width):
    items = PARTS * width
    return pl.pallas_call(
        functools.partial(gather_kernel, base=base),
        in_specs=[SMEM, SMEM, ANY, ANY, ANY, ANY, ANY],
        out_specs=[VMEM, VMEM],
        out_shape=[
            jax.ShapeDtypeStruct((PARTS, 64, width), F32),
            jax.ShapeDtypeStruct((items // 128, 128), jnp.int32),
        ],
        scratch_shapes=[
            pltpu.VMEM((BATCH * 128, 128), F32),
            pltpu.SMEM((BATCH * 128,), jnp.int32),
            pltpu.SMEM((BATCH * 128,), jnp.int32),
            pltpu.SMEM((SLOTS,), jnp.int32),
            pltpu.VMEM((SLOTS, 128), F32),
            pltpu.SemaphoreType.DMA,
            pltpu.SemaphoreType.DMA((2,)),
            pltpu.SemaphoreType.DMA((4,)),
        ],
        compiler_params=params(),
        cost_estimate=cost(items * 2000, items * 5000),
        name="gather",
    )(*lists, rows)


def tables():
    n = np.arange(256)
    angle = 2.0 * np.pi * ((n[:, None] * n[None, :]) % 256) / 256.0
    matrix = np.concatenate([np.cos(angle), np.sin(angle)], 0).astype(np.float32)
    high = matrix.astype(ml_dtypes.bfloat16)
    low = (matrix - high.astype(np.float32)).astype(ml_dtypes.bfloat16)
    matrix = np.concatenate([high, high, low], 1)
    phase = 2.0 * np.pi * np.arange(1, 4)[:, None] * n[None, :] / 1024.0
    turn = np.stack([np.cos(phase), np.sin(phase)], 1).astype(np.float32)
    return matrix, np.repeat(turn[:, :, :, None], 128, 3)


def split(values):
    high = values.astype(BF16)
    low = (values - high.astype(F32)).astype(BF16)
    return jnp.concatenate([high, low, high], 0)


def halves(ref, part, lanes):
    values = ref[:, part * 16 : part * 16 + 16, lanes].reshape(ENERGIES, -1)
    return values[:256], values[256:]


def turned(turn, r, lanes):
    repeat = (lanes.stop - lanes.start) // 128
    return [jnp.concatenate([turn[r - 1, part]] * repeat, 1) for part in range(2)]


def product(matrix, re, im):
    both = jnp.dot(matrix[...], split(jnp.concatenate([re, im], 1)), preferred_element_type=F32)
    half = re.shape[1]
    return both[:256, :half], both[:256, half:], both[256:, :half], both[256:, half:]


def lesser_kernel(matrix, turn, both_in, spectrum, both, sem):
    load = pltpu.make_async_copy(both_in.at[:, :32, :], both, sem)
    load.start()
    load.wait()
    tile = min(TILE, both.shape[-1])
    for w in range(0, both.shape[-1], tile):
        lanes = slice(w, w + tile)
        re0, re1 = halves(both, 0, lanes)
        im0, im1 = halves(both, 1, lanes)
        for r in range(4):
            re = (re0 + re1, re0 + im1, re0 - re1, re0 - im1)[r]
            im = (im0 + im1, im0 - re1, im0 - im1, im0 + re1)[r]
            if r:
                c, s = turned(turn, r, lanes)
                re, im = re * c + im * s, im * c - re * s
            cos_re, cos_im, sin_re, sin_im = product(matrix, re, im)
            spectrum[r, 0, :, lanes] = cos_re + sin_im
            spectrum[r, 1, :, lanes] = cos_im - sin_re


def lesser_spectrum(matrix, turn, both):
    width = both.shape[-1]
    return pl.pallas_call(
        lesser_kernel,
        in_specs=[VMEM, VMEM, ANY],
        out_specs=VMEM,
        out_shape=jax.ShapeDtypeStruct((4, 2, 256, width), F32),
        scratch_shapes=[pltpu.VMEM((PARTS, 32, width), F32), pltpu.SemaphoreType.DMA],
        compiler_params=params(),
        cost_estimate=cost(width * 2 * 4 * 512 * 768 * 2, width * 12288),
        name="lesser_spectrum",
    )(matrix, turn, both)


def correlate_kernel(matrix_in, turn_in, spectrum_in, b_in, out, matrix, turn, spectrum, b_ref, sems):
    first = [
        pltpu.make_async_copy(b_in, b_ref, sems.at[0]),
        pltpu.make_async_copy(matrix_in, matrix, sems.at[1]),
    ]
    loads = [pltpu.make_async_copy(spectrum_in.at[r], spectrum.at[r], sems.at[3 + r]) for r in range(4)]
    angles = pltpu.make_async_copy(turn_in, turn, sems.at[2])
    for load in first:
        load.start()
    for load in first:
        load.wait()
    loads[0].start()
    angles.start()
    for load in loads[1:]:
        load.start()
    scale = 1.0 / (1024.0 * math.sqrt(ENERGIES))
    tile = min(TILE, out.shape[-1])
    for w in range(0, out.shape[-1], tile):
        part = slice(w, w + tile)
        re0, re1 = halves(b_ref, 0, part)
        im0, im1 = halves(b_ref, 1, part)
        low_re = low_im = high_re = high_im = None
        for r in range(4):
            re = (re0 + re1, re0 - im1, re0 - re1, re0 + im1)[r]
            im = (im0 + im1, im0 + re1, im0 - im1, im0 - re1)[r]
            if r:
                if w == 0 and r == 1:
                    angles.wait()
                c, s = turned(turn, r, part)
                re, im = re * c - im * s, im * c + re * s
            cos_re, cos_im, sin_re, sin_im = product(matrix, re, im)
            b_re, b_im = cos_re - sin_im, cos_im + sin_re
            if w == 0:
                loads[r].wait()
            a_re, a_im = spectrum[r, 0, :, part], spectrum[r, 1, :, part]
            cos_re, cos_im, sin_re, sin_im = product(
                matrix, a_re * b_re - a_im * b_im, a_re * b_im + a_im * b_re
            )
            re, im = cos_re - sin_im, cos_im + sin_re
            if r:
                re, im = re * c - im * s, re * s + im * c
            if r == 0:
                low_re, low_im, high_re, high_im = re, im, re, im
            else:
                low_re, low_im = low_re + re, low_im + im
                if r == 1:
                    high_re, high_im = high_re - im, high_im + re
                elif r == 2:
                    high_re, high_im = high_re - re, high_im - im
                else:
                    high_re, high_im = high_re + im, high_im - re
        shape = (16, 16, tile)
        out[:16, :16, part] = (low_im * scale).reshape(shape)
        out[16:, :16, part] = (high_im * scale).reshape(shape)
        out[:16, 16:, part] = (low_re * -scale).reshape(shape)
        out[16:, 16:, part] = (high_re * -scale).reshape(shape)


def correlate(matrix, turn, spectrum, b):
    width = b.shape[-1]
    return pl.pallas_call(
        correlate_kernel,
        in_specs=[ANY] * 4,
        out_specs=VMEM,
        out_shape=jax.ShapeDtypeStruct((PARTS, 32, width), F32),
        scratch_shapes=[
            pltpu.VMEM(matrix.shape, BF16),
            pltpu.VMEM(turn.shape, F32),
            pltpu.VMEM(spectrum.shape, F32),
            pltpu.VMEM(b.shape, F32),
            pltpu.SemaphoreType.DMA((7,)),
        ],
        compiler_params=params(),
        cost_estimate=cost(width * 2 * 4 * 512 * 768 * 4, width * 12288),
        name="correlate",
    )(matrix, turn, spectrum, b)


def scatter_rows(row_of, column, values, out, packed, lists, list_sems):
    per = values.shape[-1] // 128
    items = BATCH * 128
    count = PARTS * per // BATCH

    def fetch(batch, h):
        piece = pl.ds(pl.multiple_of(batch * items, items), items)
        return pltpu.make_async_copy(row_of.at[piece], lists[h], list_sems.at[h])

    fetch(0, 0).start()
    fetch(1, 1).start()

    def pair(k, _):
        for h in range(2):
            batch = 2 * k + h
            blocks = []
            for b in range(BATCH):
                block = batch * BATCH + b
                w = b % per * 128
                group = (column[pl.ds(block, 1), :] >> 7) & 3
                data = values[block // per, :, w : w + 128]
                blocks.append(jnp.concatenate([jnp.where(group == g, data, 0.0) for g in range(4)], 0).T)
            for b in range(BATCH):
                packed[b * 128 : (b + 1) * 128, :] = blocks[b]
            fetch(batch, h).wait()
            for r in range(0, items, UNROLL):
                rows = [lists[h][r + u] for u in range(UNROLL)]
                for u in range(UNROLL):
                    row = packed[r + u : r + u + 1, :]
                    pltpu.store(out.at[pl.ds(rows[u], 1), :], row, mask=row != 0.0)

            @pl.when(batch + 2 < count)
            def _():
                fetch(batch + 2, h).start()

        return 0

    lax.fori_loop(0, count // 2, pair, 0)


def scatter_first_kernel(row_of, column, values, out, packed, list0, list1, list_sems, slots, sem):
    slots[...] = jnp.zeros_like(slots)
    scatter_rows(row_of, column, values, slots, packed, (list0, list1), list_sems)
    save = pltpu.make_async_copy(slots, out.at[0], sem)
    save.start()
    save.wait()


def scatter_last_kernel(
    row_of, column, values, before, out, packed, list0, list1, list_sems, slots, earlier, staged, in_sem, out_sem
):
    load = pltpu.make_async_copy(before.at[0], earlier, in_sem)
    load.start()
    slots[...] = jnp.zeros_like(slots)
    scatter_rows(row_of, column, values, slots, packed, (list0, list1), list_sems)
    load.wait()
    pieces = out_sem.shape[0]
    span = SLOTS // pieces
    copies = []
    for p in range(pieces):
        for q in range(p * span // 512, (p + 1) * span // 512):
            rows = slice(q * 128, (q + 1) * 128)
            block = (slots[rows, :] + earlier[rows, :]).T
            for g in range(4):
                s = slice(q * 512 + g * 128, q * 512 + (g + 1) * 128)
                staged[:, :, s] = block[g * 32 : (g + 1) * 32].reshape(2, 16, 128)
        piece = slice(p * span, (p + 1) * span)
        copies.append(pltpu.make_async_copy(staged.at[:, :, piece], out.at[:, :, piece], out_sem.at[p]))
        copies[-1].start()
    for copy in copies:
        copy.wait()


def scatter(columns, values, before):
    width = values.shape[-1]
    items = PARTS * width
    row_of = ((columns >> 9 << 7) | (columns & 127)).reshape(items)
    first = before is None
    scratch = [
        pltpu.VMEM((BATCH * 128, 128), F32),
        pltpu.SMEM((BATCH * 128,), jnp.int32),
        pltpu.SMEM((BATCH * 128,), jnp.int32),
        pltpu.SemaphoreType.DMA((2,)),
        pltpu.VMEM((SLOTS // 4, 128), F32),
    ]
    if first:
        scratch += [pltpu.SemaphoreType.DMA]
    else:
        scratch += [
            pltpu.VMEM((SLOTS // 4, 128), F32),
            pltpu.VMEM((2, 16, SLOTS), F32),
            pltpu.SemaphoreType.DMA,
            pltpu.SemaphoreType.DMA((8,)),
        ]
    return pl.pallas_call(
        scatter_first_kernel if first else scatter_last_kernel,
        in_specs=[ANY, VMEM, VMEM] + ([] if first else [ANY]),
        out_specs=ANY,
        out_shape=jax.ShapeDtypeStruct((6, SLOTS // 4, 128) if first else (2, 16, SLOTS), F32),
        scratch_shapes=scratch,
        compiler_params=params(44 << 20),
        cost_estimate=cost(items * 1000, items * 4000),
        name="scatter",
    )(row_of, columns, values, *(() if first else (before,)))


def local(g_lesser, g_greater, live_columns, live_count, mirror):
    slabs = lax.axis_size("slab")
    across = [(s, slabs - 1 - s) for s in range(slabs)]
    upper = (lax.axis_index("slab") >= slabs // 2).astype(jnp.int32).reshape(1)
    other_mirror = lax.ppermute(mirror, "slab", across)
    other_live = lax.ppermute(live_columns, "slab", across)
    rows, identity = column_rows(g_lesser, g_greater)
    identity = identity.reshape(SLOTS)
    lists = (live_count, upper, live_columns, other_live, identity, other_mirror)
    matrix, turn = tables()
    matrix, turn = jnp.asarray(matrix), jnp.asarray(turn)

    def swap(values):
        return lax.all_to_all(values, "energy", 0, 0, tiled=True)

    def cross(values):
        return lax.ppermute(values, "slab", across)

    picked0, columns0 = gather(lists, rows, 0, WIDTHS[0])
    picked1, columns1 = gather(lists, rows, PARTS * WIDTHS[0], WIDTHS[1])
    arrived0 = swap(picked0)
    lesser0, greater0 = arrived0[:, :32], arrived0[:, 32:]
    mirrored0 = cross(greater0)
    arrived1 = swap(picked1)
    spectrum0 = lesser_spectrum(matrix, turn, lesser0)
    arrived1, spectrum0 = lax.optimization_barrier((arrived1, spectrum0))
    mirrored1 = cross(arrived1[:, 32:])
    polar0 = swap(correlate(matrix, turn, spectrum0, mirrored0))
    spectrum1 = lesser_spectrum(matrix, turn, arrived1)
    polar1 = swap(correlate(matrix, turn, spectrum1, mirrored1))
    slots = scatter(columns0, polar0, None)
    return scatter(columns1, polar1, slots)


def solution(mesh):
    spec = jax.P(None, "energy", "slab")
    return jax.shard_map(
        local,
        mesh=mesh,
        in_specs=(spec, spec, jax.P("slab"), jax.P("slab"), jax.P("slab")),
        out_specs=spec,
        check_vma=False,
    )
```

```python
import functools
import math

import jax
import jax.numpy as jnp
import ml_dtypes
import numpy as np
from jax import lax
from jax.experimental import pallas as pl
from jax.experimental.pallas import tpu as pltpu

F32 = jnp.float32
BF16 = jnp.bfloat16
SLOTS = 32768
LIVE = 16384
ENERGIES = 512
PARTS = 32
WIDTHS = (256, 256)
VMEM_BYTES = 60 << 20
SMEM = pl.BlockSpec(memory_space=pltpu.SMEM)
VMEM = pl.BlockSpec(memory_space=pltpu.VMEM)
ANY = pl.BlockSpec(memory_space=pl.ANY)
UNROLL = 32
BATCH = 8
TILE = 256


def params(limit=VMEM_BYTES):
    return pltpu.CompilerParams(vmem_limit_bytes=limit)


def cost(flops, bytes_accessed):
    return pl.CostEstimate(flops=flops, bytes_accessed=bytes_accessed, transcendentals=0)


def rows_kernel(a_low, b_low, a_high, b_high, rows, numbers):
    number = lax.broadcasted_iota(jnp.int32, numbers.shape, 0) * 128
    numbers[...] = number + lax.broadcasted_iota(jnp.int32, numbers.shape, 1)
    for j in range(a_low.shape[-1] // 128):
        s = slice(j * 128, (j + 1) * 128)
        block = [ref[:, :, s].reshape(32, 128) for ref in (a_low, b_low, a_high, b_high)]
        rows[s, :] = jnp.concatenate(block, 0).T


def column_rows(a, b, block=4096):
    steps = LIVE // block
    low = pl.BlockSpec((2, 16, block), lambda i: (0, 0, i))
    high = pl.BlockSpec((2, 16, block), lambda i: (0, 0, i + steps))
    return pl.pallas_call(
        rows_kernel,
        grid=(steps,),
        in_specs=[low, low, high, high],
        out_specs=[
            pl.BlockSpec((block, 128), lambda i: (i, 0)),
            pl.BlockSpec((SLOTS // 128, 128), lambda i: (0, 0)),
        ],
        out_shape=[
            jax.ShapeDtypeStruct((LIVE, 128), F32),
            jax.ShapeDtypeStruct((SLOTS // 128, 128), jnp.int32),
        ],
        compiler_params=params(),
        cost_estimate=cost(1 << 20, 24 << 20),
        name="column_rows",
    )(a, b, a, b)


def gather_kernel(
    count, upper, own, other, identity, mirror, rows, out, places,
    packed, list0, list1, mapped, table, map_sem, list_sems, row_sems, *, base
):
    width = out.shape[-1]
    per = width // 128
    lists = (list0, list1)
    items = BATCH * 128
    count_batches = PARTS * per // BATCH

    def fetch(source, batch, h):
        piece = pl.ds(pl.multiple_of(base + batch * items, items), items)
        return pltpu.make_async_copy(source.at[piece], lists[h], list_sems.at[h])

    def start(batch, h):
        @pl.when(upper[0] == 0)
        def _():
            fetch(own, batch, h).start()

        @pl.when(upper[0] != 0)
        def _():
            fetch(other, batch, h).start()

    @pl.when(upper[0] == 0)
    def _():
        pltpu.make_async_copy(identity, mapped, map_sem).start()

    @pl.when(upper[0] != 0)
    def _():
        pltpu.make_async_copy(mirror, mapped, map_sem).start()

    start(0, 0)
    start(1, 1)
    parts = row_sems.shape[0]
    span = LIVE // parts
    loads = []
    for p in range(parts):
        s = pl.ds(p * span, span)
        loads.append(pltpu.make_async_copy(rows.at[s, :], table.at[s, :], row_sems.at[p]))
    for copy in loads:
        copy.start()
    step = 2048
    first_half = lax.broadcasted_iota(jnp.int32, (8, 128), 1) < 64
    number = lax.broadcasted_iota(jnp.int32, (8, 128), 0).astype(F32)
    for p in range(parts):
        loads[p].wait()

        def widen(k, _):
            first = pl.multiple_of(p * span + k * step, step)
            offset = number + first.astype(F32)
            for r in range(0, step, 8):
                both = table[pl.ds(first + r, 8), :]
                high = pltpu.roll(both, 64, 1)
                column = offset + float(r)
                table[pl.ds(first + r, 8), :] = jnp.where(first_half, both, column)
                table[pl.ds(first + r + LIVE, 8), :] = jnp.where(first_half, high, column + float(LIVE))
            return 0

        lax.fori_loop(0, span // step, widen, 0)
    pltpu.make_async_copy(identity, mapped, map_sem).wait()
    lane = lax.broadcasted_iota(jnp.int32, (1, 128), 1)

    def pair(k, _):
        for h in range(2):
            batch = 2 * k + h
            fetch(own, batch, h).wait()
            for r in range(0, items, UNROLL):
                cols = [mapped[lists[h][r + u]] for u in range(UNROLL)]
                for u in range(UNROLL):
                    packed[r + u : r + u + 1, :] = table[pl.ds(cols[u], 1), :]

            @pl.when(batch + 2 < count_batches)
            def _():
                start(batch + 2, h)

            blocks = [packed[b * 128 : (b + 1) * 128, :].T for b in range(BATCH)]
            for b in range(BATCH):
                block = batch * BATCH + b
                w = b % per * 128
                live = lane + (block * 128 + base) < count[0]
                out[block // per, :, w : w + 128] = jnp.where(live, blocks[b][:64], 0.0)
                places[pl.ds(block, 1), :] = blocks[b][64:65].astype(jnp.int32)
        return 0

    lax.fori_loop(0, count_batches // 2, pair, 0)


def gather(lists, rows, base, width):
    items = PARTS * width
    return pl.pallas_call(
        functools.partial(gather_kernel, base=base),
        in_specs=[SMEM, SMEM, ANY, ANY, ANY, ANY, ANY],
        out_specs=[VMEM, VMEM],
        out_shape=[
            jax.ShapeDtypeStruct((PARTS, 64, width), F32),
            jax.ShapeDtypeStruct((items // 128, 128), jnp.int32),
        ],
        scratch_shapes=[
            pltpu.VMEM((BATCH * 128, 128), F32),
            pltpu.SMEM((BATCH * 128,), jnp.int32),
            pltpu.SMEM((BATCH * 128,), jnp.int32),
            pltpu.SMEM((SLOTS,), jnp.int32),
            pltpu.VMEM((SLOTS, 128), F32),
            pltpu.SemaphoreType.DMA,
            pltpu.SemaphoreType.DMA((2,)),
            pltpu.SemaphoreType.DMA((4,)),
        ],
        compiler_params=params(),
        cost_estimate=cost(items * 2000, items * 5000),
        name="gather",
    )(*lists, rows)


def tables():
    n = np.arange(256)
    angle = 2.0 * np.pi * ((n[:, None] * n[None, :]) % 256) / 256.0
    matrix = np.concatenate([np.cos(angle), np.sin(angle)], 0).astype(np.float32)
    high = matrix.astype(ml_dtypes.bfloat16)
    low = (matrix - high.astype(np.float32)).astype(ml_dtypes.bfloat16)
    matrix = np.concatenate([high, high, low], 1)
    phase = 2.0 * np.pi * np.arange(1, 4)[:, None] * n[None, :] / 1024.0
    turn = np.stack([np.cos(phase), np.sin(phase)], 1).astype(np.float32)
    return matrix, np.repeat(turn[:, :, :, None], 128, 3)


def split(values):
    high = values.astype(BF16)
    low = (values - high.astype(F32)).astype(BF16)
    return jnp.concatenate([high, low, high], 0)


def halves(ref, part, lanes):
    values = ref[:, part * 16 : part * 16 + 16, lanes].reshape(ENERGIES, -1)
    return values[:256], values[256:]


def turned(turn, r, lanes):
    repeat = (lanes.stop - lanes.start) // 128
    return [jnp.concatenate([turn[r - 1, part]] * repeat, 1) for part in range(2)]


def product(matrix, re, im):
    both = jnp.dot(matrix[...], split(jnp.concatenate([re, im], 1)), preferred_element_type=F32)
    half = re.shape[1]
    return both[:256, :half], both[:256, half:], both[256:, :half], both[256:, half:]


def lesser_kernel(matrix, turn, both_in, spectrum, both, sem):
    load = pltpu.make_async_copy(both_in.at[:, :32, :], both, sem)
    load.start()
    load.wait()
    tile = min(TILE, both.shape[-1])
    for w in range(0, both.shape[-1], tile):
        lanes = slice(w, w + tile)
        re0, re1 = halves(both, 0, lanes)
        im0, im1 = halves(both, 1, lanes)
        for r in range(4):
            re = (re0 + re1, re0 + im1, re0 - re1, re0 - im1)[r]
            im = (im0 + im1, im0 - re1, im0 - im1, im0 + re1)[r]
            if r:
                c, s = turned(turn, r, lanes)
                re, im = re * c + im * s, im * c - re * s
            cos_re, cos_im, sin_re, sin_im = product(matrix, re, im)
            spectrum[r, 0, :, lanes] = cos_re + sin_im
            spectrum[r, 1, :, lanes] = cos_im - sin_re


def lesser_spectrum(matrix, turn, both, limit):
    width = both.shape[-1]
    return pl.pallas_call(
        lesser_kernel,
        in_specs=[VMEM, VMEM, ANY],
        out_specs=VMEM,
        out_shape=jax.ShapeDtypeStruct((4, 2, 256, width), F32),
        scratch_shapes=[pltpu.VMEM((PARTS, 32, width), F32), pltpu.SemaphoreType.DMA],
        compiler_params=params(limit << 20),
        cost_estimate=cost(width * 2 * 4 * 512 * 768 * 2, width * 12288),
        name="lesser_spectrum",
    )(matrix, turn, both)


def correlate_kernel(matrix, turn, spectrum, b_ref, out):
    scale = 1.0 / (1024.0 * math.sqrt(ENERGIES))
    tile = min(TILE, out.shape[-1])
    for w in range(0, out.shape[-1], tile):
        part = slice(w, w + tile)
        re0, re1 = halves(b_ref, 0, part)
        im0, im1 = halves(b_ref, 1, part)
        low_re = low_im = high_re = high_im = None
        for r in range(4):
            re = (re0 + re1, re0 - im1, re0 - re1, re0 + im1)[r]
            im = (im0 + im1, im0 + re1, im0 - im1, im0 - re1)[r]
            if r:
                c, s = turned(turn, r, part)
                re, im = re * c - im * s, im * c + re * s
            cos_re, cos_im, sin_re, sin_im = product(matrix, re, im)
            b_re, b_im = cos_re - sin_im, cos_im + sin_re
            a_re, a_im = spectrum[r, 0, :, part], spectrum[r, 1, :, part]
            cos_re, cos_im, sin_re, sin_im = product(
                matrix, a_re * b_re - a_im * b_im, a_re * b_im + a_im * b_re
            )
            re, im = cos_re - sin_im, cos_im + sin_re
            if r:
                re, im = re * c - im * s, re * s + im * c
            if r == 0:
                low_re, low_im, high_re, high_im = re, im, re, im
            else:
                low_re, low_im = low_re + re, low_im + im
                if r == 1:
                    high_re, high_im = high_re - im, high_im + re
                elif r == 2:
                    high_re, high_im = high_re - re, high_im - im
                else:
                    high_re, high_im = high_re + im, high_im - re
        shape = (16, 16, tile)
        out[:16, :16, part] = (low_im * scale).reshape(shape)
        out[16:, :16, part] = (high_im * scale).reshape(shape)
        out[:16, 16:, part] = (low_re * -scale).reshape(shape)
        out[16:, 16:, part] = (high_re * -scale).reshape(shape)


def correlate(matrix, turn, spectrum, b, limit):
    width = b.shape[-1]
    return pl.pallas_call(
        correlate_kernel,
        in_specs=[VMEM] * 4,
        out_specs=VMEM,
        out_shape=jax.ShapeDtypeStruct((PARTS, 32, width), F32),
        compiler_params=params(limit << 20),
        cost_estimate=cost(width * 2 * 4 * 512 * 768 * 4, width * 12288),
        name="correlate",
    )(matrix, turn, spectrum, b)


def scatter_rows(row_of, column, values, out, packed, lists, list_sems):
    per = values.shape[-1] // 128
    items = BATCH * 128
    count = PARTS * per // BATCH

    def fetch(batch, h):
        piece = pl.ds(pl.multiple_of(batch * items, items), items)
        return pltpu.make_async_copy(row_of.at[piece], lists[h], list_sems.at[h])

    fetch(0, 0).start()
    fetch(1, 1).start()

    def pair(k, _):
        for h in range(2):
            batch = 2 * k + h
            blocks = []
            for b in range(BATCH):
                block = batch * BATCH + b
                w = b % per * 128
                group = (column[pl.ds(block, 1), :] >> 7) & 3
                data = values[block // per, :, w : w + 128]
                blocks.append(jnp.concatenate([jnp.where(group == g, data, 0.0) for g in range(4)], 0).T)
            for b in range(BATCH):
                packed[b * 128 : (b + 1) * 128, :] = blocks[b]
            fetch(batch, h).wait()
            for r in range(0, items, UNROLL):
                rows = [lists[h][r + u] for u in range(UNROLL)]
                for u in range(UNROLL):
                    row = packed[r + u : r + u + 1, :]
                    pltpu.store(out.at[pl.ds(rows[u], 1), :], row, mask=row != 0.0)

            @pl.when(batch + 2 < count)
            def _():
                fetch(batch + 2, h).start()

        return 0

    lax.fori_loop(0, count // 2, pair, 0)


def scatter_first_kernel(row_of, column, values, out, packed, list0, list1, list_sems, slots, sem):
    slots[...] = jnp.zeros_like(slots)
    scatter_rows(row_of, column, values, slots, packed, (list0, list1), list_sems)
    save = pltpu.make_async_copy(slots, out.at[0], sem)
    save.start()
    save.wait()


def scatter_last_kernel(
    row_of, column, values, before, out, packed, list0, list1, list_sems, slots, earlier, staged, in_sem, out_sem
):
    load = pltpu.make_async_copy(before.at[0], earlier, in_sem)
    load.start()
    slots[...] = jnp.zeros_like(slots)
    scatter_rows(row_of, column, values, slots, packed, (list0, list1), list_sems)
    load.wait()
    pieces = out_sem.shape[0]
    span = SLOTS // pieces
    copies = []
    for p in range(pieces):
        for q in range(p * span // 512, (p + 1) * span // 512):
            rows = slice(q * 128, (q + 1) * 128)
            block = (slots[rows, :] + earlier[rows, :]).T
            for g in range(4):
                s = slice(q * 512 + g * 128, q * 512 + (g + 1) * 128)
                staged[:, :, s] = block[g * 32 : (g + 1) * 32].reshape(2, 16, 128)
        piece = slice(p * span, (p + 1) * span)
        copies.append(pltpu.make_async_copy(staged.at[:, :, piece], out.at[:, :, piece], out_sem.at[p]))
        copies[-1].start()
    for copy in copies:
        copy.wait()


def scatter(columns, values, before):
    width = values.shape[-1]
    items = PARTS * width
    row_of = ((columns >> 9 << 7) | (columns & 127)).reshape(items)
    first = before is None
    scratch = [
        pltpu.VMEM((BATCH * 128, 128), F32),
        pltpu.SMEM((BATCH * 128,), jnp.int32),
        pltpu.SMEM((BATCH * 128,), jnp.int32),
        pltpu.SemaphoreType.DMA((2,)),
        pltpu.VMEM((SLOTS // 4, 128), F32),
    ]
    if first:
        scratch += [pltpu.SemaphoreType.DMA]
    else:
        scratch += [
            pltpu.VMEM((SLOTS // 4, 128), F32),
            pltpu.VMEM((2, 16, SLOTS), F32),
            pltpu.SemaphoreType.DMA,
            pltpu.SemaphoreType.DMA((8,)),
        ]
    return pl.pallas_call(
        scatter_first_kernel if first else scatter_last_kernel,
        in_specs=[ANY, VMEM, VMEM] + ([] if first else [ANY]),
        out_specs=ANY,
        out_shape=jax.ShapeDtypeStruct((6, SLOTS // 4, 128) if first else (2, 16, SLOTS), F32),
        scratch_shapes=scratch,
        compiler_params=params(44 << 20),
        cost_estimate=cost(items * 1000, items * 4000),
        name="scatter",
    )(row_of, columns, values, *(() if first else (before,)))


def local(g_lesser, g_greater, live_columns, live_count, mirror):
    slabs = lax.axis_size("slab")
    across = [(s, slabs - 1 - s) for s in range(slabs)]
    upper = (lax.axis_index("slab") >= slabs // 2).astype(jnp.int32).reshape(1)
    other_mirror = lax.ppermute(mirror, "slab", across)
    other_live = lax.ppermute(live_columns, "slab", across)
    rows, identity = column_rows(g_lesser, g_greater)
    identity = identity.reshape(SLOTS)
    lists = (live_count, upper, live_columns, other_live, identity, other_mirror)
    matrix, turn = tables()
    matrix, turn = jnp.asarray(matrix), jnp.asarray(turn)

    def swap(values):
        return lax.all_to_all(values, "energy", 0, 0, tiled=True)

    def cross(values):
        return lax.ppermute(values, "slab", across)

    picked0, columns0 = gather(lists, rows, 0, WIDTHS[0])
    picked1, columns1 = gather(lists, rows, PARTS * WIDTHS[0], WIDTHS[1])
    arrived0 = swap(picked0)
    lesser0, greater0 = arrived0[:, :32], arrived0[:, 32:]
    mirrored0 = cross(greater0)
    arrived1 = swap(picked1)
    spectrum0 = lesser_spectrum(matrix, turn, lesser0, 60)
    arrived1, spectrum0 = lax.optimization_barrier((arrived1, spectrum0))
    mirrored1 = cross(arrived1[:, 32:])
    polar0 = swap(correlate(matrix, turn, spectrum0, mirrored0, 50))
    spectrum1 = lesser_spectrum(matrix, turn, arrived1, 50)
    polar1 = swap(correlate(matrix, turn, spectrum1, mirrored1, 50))
    slots = scatter(columns0, polar0, None)
    return scatter(columns1, polar1, slots)


def solution(mesh):
    spec = jax.P(None, "energy", "slab")
    return jax.shard_map(
        local,
        mesh=mesh,
        in_specs=(spec, spec, jax.P("slab"), jax.P("slab"), jax.P("slab")),
        out_specs=spec,
        check_vma=False,
    )
```

```python
import functools
import math

import jax
import jax.numpy as jnp
import ml_dtypes
import numpy as np
from jax import lax
from jax.experimental import pallas as pl
from jax.experimental.pallas import tpu as pltpu

F32 = jnp.float32
BF16 = jnp.bfloat16
SLOTS = 32768
LIVE = 16384
ENERGIES = 512
PARTS = 32
WIDTHS = (256, 256)
VMEM_BYTES = 60 << 20
SMEM = pl.BlockSpec(memory_space=pltpu.SMEM)
VMEM = pl.BlockSpec(memory_space=pltpu.VMEM)
ANY = pl.BlockSpec(memory_space=pl.ANY)
UNROLL = 32
BATCH = 8
TILE = 256


def params(limit=VMEM_BYTES):
    return pltpu.CompilerParams(vmem_limit_bytes=limit)


def cost(flops, bytes_accessed):
    return pl.CostEstimate(flops=flops, bytes_accessed=bytes_accessed, transcendentals=0)


def rows_kernel(a_low, b_low, a_high, b_high, rows, numbers):
    number = lax.broadcasted_iota(jnp.int32, numbers.shape, 0) * 128
    numbers[...] = number + lax.broadcasted_iota(jnp.int32, numbers.shape, 1)
    for j in range(a_low.shape[-1] // 128):
        s = slice(j * 128, (j + 1) * 128)
        block = [ref[:, :, s].reshape(32, 128) for ref in (a_low, b_low, a_high, b_high)]
        rows[s, :] = jnp.concatenate(block, 0).T


def column_rows(a, b, block=4096):
    steps = LIVE // block
    low = pl.BlockSpec((2, 16, block), lambda i: (0, 0, i))
    high = pl.BlockSpec((2, 16, block), lambda i: (0, 0, i + steps))
    return pl.pallas_call(
        rows_kernel,
        grid=(steps,),
        in_specs=[low, low, high, high],
        out_specs=[
            pl.BlockSpec((block, 128), lambda i: (i, 0)),
            pl.BlockSpec((SLOTS // 128, 128), lambda i: (0, 0)),
        ],
        out_shape=[
            jax.ShapeDtypeStruct((LIVE, 128), F32),
            jax.ShapeDtypeStruct((SLOTS // 128, 128), jnp.int32),
        ],
        compiler_params=params(),
        cost_estimate=cost(1 << 20, 24 << 20),
        name="column_rows",
    )(a, b, a, b)


def gather_kernel(
    count, upper, own, other, identity, rows, out, places,
    packed, list0, list1, mapped, table, map_sem, list_sems, row_sems, *, base
):
    width = out.shape[-1]
    per = width // 128
    lists = (list0, list1)
    items = BATCH * 128
    count_batches = PARTS * per // BATCH

    def fetch(source, batch, h, skip=0):
        piece = pl.ds(pl.multiple_of(skip + base + batch * items, items), items)
        return pltpu.make_async_copy(source.at[piece], lists[h], list_sems.at[h])

    def start(batch, h):
        @pl.when(upper[0] == 0)
        def _():
            fetch(own, batch, h).start()

        @pl.when(upper[0] != 0)
        def _():
            fetch(other, batch, h, SLOTS).start()

    @pl.when(upper[0] == 0)
    def _():
        pltpu.make_async_copy(identity, mapped, map_sem).start()

    @pl.when(upper[0] != 0)
    def _():
        pltpu.make_async_copy(other.at[pl.ds(0, SLOTS)], mapped, map_sem).start()

    start(0, 0)
    start(1, 1)
    parts = row_sems.shape[0]
    span = LIVE // parts
    loads = []
    for p in range(parts):
        s = pl.ds(p * span, span)
        loads.append(pltpu.make_async_copy(rows.at[s, :], table.at[s, :], row_sems.at[p]))
    for copy in loads:
        copy.start()
    step = 2048
    first_half = lax.broadcasted_iota(jnp.int32, (8, 128), 1) < 64
    number = lax.broadcasted_iota(jnp.int32, (8, 128), 0).astype(F32)
    for p in range(parts):
        loads[p].wait()

        def widen(k, _):
            first = pl.multiple_of(p * span + k * step, step)
            offset = number + first.astype(F32)
            for r in range(0, step, 8):
                both = table[pl.ds(first + r, 8), :]
                high = pltpu.roll(both, 64, 1)
                column = offset + float(r)
                table[pl.ds(first + r, 8), :] = jnp.where(first_half, both, column)
                table[pl.ds(first + r + LIVE, 8), :] = jnp.where(first_half, high, column + float(LIVE))
            return 0

        lax.fori_loop(0, span // step, widen, 0)
    pltpu.make_async_copy(identity, mapped, map_sem).wait()
    lane = lax.broadcasted_iota(jnp.int32, (1, 128), 1)

    def pair(k, _):
        for h in range(2):
            batch = 2 * k + h
            fetch(own, batch, h).wait()
            for r in range(0, items, UNROLL):
                cols = [mapped[lists[h][r + u]] for u in range(UNROLL)]
                for u in range(UNROLL):
                    packed[r + u : r + u + 1, :] = table[pl.ds(cols[u], 1), :]

            @pl.when(batch + 2 < count_batches)
            def _():
                start(batch + 2, h)

            blocks = [packed[b * 128 : (b + 1) * 128, :].T for b in range(BATCH)]
            for b in range(BATCH):
                block = batch * BATCH + b
                w = b % per * 128
                live = lane + (block * 128 + base) < count[0]
                out[block // per, :, w : w + 128] = jnp.where(live, blocks[b][:64], 0.0)
                places[pl.ds(block, 1), :] = blocks[b][64:65].astype(jnp.int32)
        return 0

    lax.fori_loop(0, count_batches // 2, pair, 0)


def gather(lists, rows, base, width):
    items = PARTS * width
    return pl.pallas_call(
        functools.partial(gather_kernel, base=base),
        in_specs=[SMEM, SMEM, ANY, ANY, ANY, ANY],
        out_specs=[VMEM, VMEM],
        out_shape=[
            jax.ShapeDtypeStruct((PARTS, 64, width), F32),
            jax.ShapeDtypeStruct((items // 128, 128), jnp.int32),
        ],
        scratch_shapes=[
            pltpu.VMEM((BATCH * 128, 128), F32),
            pltpu.SMEM((BATCH * 128,), jnp.int32),
            pltpu.SMEM((BATCH * 128,), jnp.int32),
            pltpu.SMEM((SLOTS,), jnp.int32),
            pltpu.VMEM((SLOTS, 128), F32),
            pltpu.SemaphoreType.DMA,
            pltpu.SemaphoreType.DMA((2,)),
            pltpu.SemaphoreType.DMA((4,)),
        ],
        compiler_params=params(),
        cost_estimate=cost(items * 2000, items * 5000),
        name="gather",
    )(*lists, rows)


def tables():
    n = np.arange(256)
    angle = 2.0 * np.pi * ((n[:, None] * n[None, :]) % 256) / 256.0
    matrix = np.concatenate([np.cos(angle), np.sin(angle)], 0).astype(np.float32)
    high = matrix.astype(ml_dtypes.bfloat16)
    low = (matrix - high.astype(np.float32)).astype(ml_dtypes.bfloat16)
    matrix = np.concatenate([high, high, low], 1)
    phase = 2.0 * np.pi * np.arange(1, 4)[:, None] * n[None, :] / 1024.0
    turn = np.stack([np.cos(phase), np.sin(phase)], 1).astype(np.float32)
    return matrix, np.repeat(turn[:, :, :, None], 128, 3)


def split(values):
    high = values.astype(BF16)
    low = (values - high.astype(F32)).astype(BF16)
    return jnp.concatenate([high, low, high], 0)


def halves(ref, part, lanes):
    values = ref[:, part * 16 : part * 16 + 16, lanes].reshape(ENERGIES, -1)
    return values[:256], values[256:]


def turned(turn, r, lanes):
    repeat = (lanes.stop - lanes.start) // 128
    return [jnp.concatenate([turn[r - 1, part]] * repeat, 1) for part in range(2)]


def product(matrix, re, im):
    both = jnp.dot(matrix[...], split(jnp.concatenate([re, im], 1)), preferred_element_type=F32)
    half = re.shape[1]
    return both[:256, :half], both[:256, half:], both[256:, :half], both[256:, half:]


def lesser_kernel(matrix, turn, both_in, spectrum, both, sem):
    load = pltpu.make_async_copy(both_in.at[:, :32, :], both, sem)
    load.start()
    load.wait()
    tile = min(TILE, both.shape[-1])
    for w in range(0, both.shape[-1], tile):
        lanes = slice(w, w + tile)
        re0, re1 = halves(both, 0, lanes)
        im0, im1 = halves(both, 1, lanes)
        for r in range(4):
            re = (re0 + re1, re0 + im1, re0 - re1, re0 - im1)[r]
            im = (im0 + im1, im0 - re1, im0 - im1, im0 + re1)[r]
            if r:
                c, s = turned(turn, r, lanes)
                re, im = re * c + im * s, im * c - re * s
            cos_re, cos_im, sin_re, sin_im = product(matrix, re, im)
            spectrum[r, 0, :, lanes] = cos_re + sin_im
            spectrum[r, 1, :, lanes] = cos_im - sin_re


def lesser_spectrum(matrix, turn, both, limit):
    width = both.shape[-1]
    return pl.pallas_call(
        lesser_kernel,
        in_specs=[VMEM, VMEM, ANY],
        out_specs=VMEM,
        out_shape=jax.ShapeDtypeStruct((4, 2, 256, width), F32),
        scratch_shapes=[pltpu.VMEM((PARTS, 32, width), F32), pltpu.SemaphoreType.DMA],
        compiler_params=params(limit << 20),
        cost_estimate=cost(width * 2 * 4 * 512 * 768 * 2, width * 12288),
        name="lesser_spectrum",
    )(matrix, turn, both)


def correlate_kernel(matrix, turn, spectrum, b_ref, out):
    scale = 1.0 / (1024.0 * math.sqrt(ENERGIES))
    tile = min(TILE, out.shape[-1])
    for w in range(0, out.shape[-1], tile):
        part = slice(w, w + tile)
        re0, re1 = halves(b_ref, 0, part)
        im0, im1 = halves(b_ref, 1, part)
        low_re = low_im = high_re = high_im = None
        for r in range(4):
            re = (re0 + re1, re0 - im1, re0 - re1, re0 + im1)[r]
            im = (im0 + im1, im0 + re1, im0 - im1, im0 - re1)[r]
            if r:
                c, s = turned(turn, r, part)
                re, im = re * c - im * s, im * c + re * s
            cos_re, cos_im, sin_re, sin_im = product(matrix, re, im)
            b_re, b_im = cos_re - sin_im, cos_im + sin_re
            a_re, a_im = spectrum[r, 0, :, part], spectrum[r, 1, :, part]
            cos_re, cos_im, sin_re, sin_im = product(
                matrix, a_re * b_re - a_im * b_im, a_re * b_im + a_im * b_re
            )
            re, im = cos_re - sin_im, cos_im + sin_re
            if r:
                re, im = re * c - im * s, re * s + im * c
            if r == 0:
                low_re, low_im, high_re, high_im = re, im, re, im
            else:
                low_re, low_im = low_re + re, low_im + im
                if r == 1:
                    high_re, high_im = high_re - im, high_im + re
                elif r == 2:
                    high_re, high_im = high_re - re, high_im - im
                else:
                    high_re, high_im = high_re + im, high_im - re
        shape = (16, 16, tile)
        out[:16, :16, part] = (low_im * scale).reshape(shape)
        out[16:, :16, part] = (high_im * scale).reshape(shape)
        out[:16, 16:, part] = (low_re * -scale).reshape(shape)
        out[16:, 16:, part] = (high_re * -scale).reshape(shape)


def correlate(matrix, turn, spectrum, b, limit):
    width = b.shape[-1]
    return pl.pallas_call(
        correlate_kernel,
        in_specs=[VMEM] * 4,
        out_specs=VMEM,
        out_shape=jax.ShapeDtypeStruct((PARTS, 32, width), F32),
        compiler_params=params(limit << 20),
        cost_estimate=cost(width * 2 * 4 * 512 * 768 * 4, width * 12288),
        name="correlate",
    )(matrix, turn, spectrum, b)


def scatter_rows(row_of, column, values, out, packed, lists, list_sems):
    per = values.shape[-1] // 128
    items = BATCH * 128
    count = PARTS * per // BATCH

    def fetch(batch, h):
        piece = pl.ds(pl.multiple_of(batch * items, items), items)
        return pltpu.make_async_copy(row_of.at[piece], lists[h], list_sems.at[h])

    fetch(0, 0).start()
    fetch(1, 1).start()

    def pair(k, _):
        for h in range(2):
            batch = 2 * k + h
            blocks = []
            for b in range(BATCH):
                block = batch * BATCH + b
                w = b % per * 128
                group = (column[pl.ds(block, 1), :] >> 7) & 3
                data = values[block // per, :, w : w + 128]
                blocks.append(jnp.concatenate([jnp.where(group == g, data, 0.0) for g in range(4)], 0).T)
            for b in range(BATCH):
                packed[b * 128 : (b + 1) * 128, :] = blocks[b]
            fetch(batch, h).wait()
            for r in range(0, items, UNROLL):
                rows = [lists[h][r + u] for u in range(UNROLL)]
                for u in range(UNROLL):
                    row = packed[r + u : r + u + 1, :]
                    pltpu.store(out.at[pl.ds(rows[u], 1), :], row, mask=row != 0.0)

            @pl.when(batch + 2 < count)
            def _():
                fetch(batch + 2, h).start()

        return 0

    lax.fori_loop(0, count // 2, pair, 0)


def scatter_first_kernel(row_of, column, values, out, packed, list0, list1, list_sems, slots, sem):
    slots[...] = jnp.zeros_like(slots)
    scatter_rows(row_of, column, values, slots, packed, (list0, list1), list_sems)
    save = pltpu.make_async_copy(slots, out.at[0], sem)
    save.start()
    save.wait()


def scatter_last_kernel(
    row_of, column, values, before, out, packed, list0, list1, list_sems, slots, earlier, staged, in_sem, out_sem
):
    load = pltpu.make_async_copy(before.at[0], earlier, in_sem)
    load.start()
    slots[...] = jnp.zeros_like(slots)
    scatter_rows(row_of, column, values, slots, packed, (list0, list1), list_sems)
    load.wait()
    pieces = out_sem.shape[0]
    span = SLOTS // pieces
    copies = []
    for p in range(pieces):
        for q in range(p * span // 512, (p + 1) * span // 512):
            rows = slice(q * 128, (q + 1) * 128)
            block = (slots[rows, :] + earlier[rows, :]).T
            for g in range(4):
                s = slice(q * 512 + g * 128, q * 512 + (g + 1) * 128)
                staged[:, :, s] = block[g * 32 : (g + 1) * 32].reshape(2, 16, 128)
        piece = slice(p * span, (p + 1) * span)
        copies.append(pltpu.make_async_copy(staged.at[:, :, piece], out.at[:, :, piece], out_sem.at[p]))
        copies[-1].start()
    for copy in copies:
        copy.wait()


def scatter(columns, values, before):
    width = values.shape[-1]
    items = PARTS * width
    row_of = ((columns >> 9 << 7) | (columns & 127)).reshape(items)
    first = before is None
    scratch = [
        pltpu.VMEM((BATCH * 128, 128), F32),
        pltpu.SMEM((BATCH * 128,), jnp.int32),
        pltpu.SMEM((BATCH * 128,), jnp.int32),
        pltpu.SemaphoreType.DMA((2,)),
        pltpu.VMEM((SLOTS // 4, 128), F32),
    ]
    if first:
        scratch += [pltpu.SemaphoreType.DMA]
    else:
        scratch += [
            pltpu.VMEM((SLOTS // 4, 128), F32),
            pltpu.VMEM((2, 16, SLOTS), F32),
            pltpu.SemaphoreType.DMA,
            pltpu.SemaphoreType.DMA((8,)),
        ]
    return pl.pallas_call(
        scatter_first_kernel if first else scatter_last_kernel,
        in_specs=[ANY, VMEM, VMEM] + ([] if first else [ANY]),
        out_specs=ANY,
        out_shape=jax.ShapeDtypeStruct((6, SLOTS // 4, 128) if first else (2, 16, SLOTS), F32),
        scratch_shapes=scratch,
        compiler_params=params(44 << 20),
        cost_estimate=cost(items * 1000, items * 4000),
        name="scatter",
    )(row_of, columns, values, *(() if first else (before,)))


def local(g_lesser, g_greater, live_columns, live_count, mirror):
    slabs = lax.axis_size("slab")
    across = [(s, slabs - 1 - s) for s in range(slabs)]
    upper = (lax.axis_index("slab") >= slabs // 2).astype(jnp.int32).reshape(1)
    other = lax.ppermute(jnp.concatenate([mirror, live_columns]), "slab", across)
    rows, identity = column_rows(g_lesser, g_greater)
    identity = identity.reshape(SLOTS)
    lists = (live_count, upper, live_columns, other, identity)
    matrix, turn = tables()
    matrix, turn = jnp.asarray(matrix), jnp.asarray(turn)

    def swap(values):
        return lax.all_to_all(values, "energy", 0, 0, tiled=True)

    def cross(values):
        return lax.ppermute(values, "slab", across)

    picked0, columns0 = gather(lists, rows, 0, WIDTHS[0])
    picked1, columns1 = gather(lists, rows, PARTS * WIDTHS[0], WIDTHS[1])
    arrived0 = swap(picked0)
    lesser0, greater0 = arrived0[:, :32], arrived0[:, 32:]
    mirrored0 = cross(greater0)
    arrived1 = swap(picked1)
    spectrum0 = lesser_spectrum(matrix, turn, lesser0, 60)
    arrived1, spectrum0 = lax.optimization_barrier((arrived1, spectrum0))
    mirrored1 = cross(arrived1[:, 32:])
    polar0 = swap(correlate(matrix, turn, spectrum0, mirrored0, 50))
    spectrum1 = lesser_spectrum(matrix, turn, arrived1, 50)
    polar1 = swap(correlate(matrix, turn, spectrum1, mirrored1, 50))
    slots = scatter(columns0, polar0, None)
    return scatter(columns1, polar1, slots)


def solution(mesh):
    spec = jax.P(None, "energy", "slab")
    return jax.shard_map(
        local,
        mesh=mesh,
        in_specs=(spec, spec, jax.P("slab"), jax.P("slab"), jax.P("slab")),
        out_specs=spec,
        check_vma=False,
    )
```
